768 devices in a mesh: dp: 96 (over x, y_lo, z), group: 8 (over y_hi, core).
Axes of the slice: x: 4, y: 8 (y_hi: 4, y_lo: 2; y = y_hi * 2 + y_lo), z: 12, core: 2. Of those that a mesh axis runs over, the one named last changes fastest.
Arguments:
- image_emb: bfloat16 [196608, 1152], P(('dp', 'group')), may hold values from -0.17675781 to 0.17675781
- text_emb: float32 [196608, 1152], P(('dp', 'group')), may hold values from -0.17677669 to 0.17677669
- text_accum: float32 [196608, 1152], P(('dp', 'group')), may hold values from -6 to 6
- pair_ids: int32 [196608], P(('dp', 'group')), may hold values from 0 to 127
- log_scale: float32 [1], replicated, may hold values from 1 to 2
- bias: float32 [1], replicated, may hold values from -3 to 0
Outputs:
- row_loss: float32 [196608], P(('dp', 'group'))
- image_grad: bfloat16 [196608, 1152], P(('dp', 'group'))
- text_grad: float32 [196608, 1152], P(('dp', 'group'))
The draws below stay inside these ranges and needn't reach their ends.
Inputs may be any that keep to these rules, and one draw needn't show every extreme that they name: `pair_ids`: two examples form a positive pair exactly where their ids are equal.
All inputs are finite; a program needn't handle non-finite values.
Results may differ from the reference program's by a relative error of at most 0.0059.
Values may be sent and summed in bfloat16 or wider, within the bound.
A program may use at most 32 MiB of HBM per device.

```python
import jax
import jax.numpy as jnp
from jax import lax

D = 1152
TOK_DEV = 256
SHIFTS = 2
TOKENS = 196608


def set_ends(values, own_key, low, largest):
    longest = values.shape.index(max(values.shape))
    spots = []
    for shift in (0, 1):
        where = [jax.random.randint(jax.random.fold_in(own_key, axis), (), 0, length) for axis, length in enumerate(values.shape)]
        where[longest] = (where[longest] + shift) % values.shape[longest]
        spots.append(tuple(where))
    return values.at[spots[0]].set(low).at[spots[1]].set(largest)


def levels(own_key, extent, shards, least, top_value):
    def one(axis_at, blocks):
        draws = jax.random.uniform(jax.random.fold_in(jax.random.fold_in(own_key, 6), axis_at), (blocks,), jnp.float32, least / len(shards), top_value / len(shards))
        return jnp.repeat(jnp.exp(draws), extent[axis_at] // blocks).reshape((-1,) + (1,) * (len(extent) - axis_at - 1))

    gain = one(*shards[0])
    for cut in shards[1:]:
        gain = gain * one(*cut)
    return gain


def centred(stream_key, extent, deviation, most, cuts=(), kind=jnp.bfloat16):
    drawn = jax.random.normal(stream_key, extent, jnp.float32) * deviation
    if len(cuts) > 0:
        drawn = levels(stream_key, extent, cuts, -0.22, 0.18) * drawn
    return jnp.clip(drawn, min=-most, max=most).astype(kind)


def setup_inputs(seed: int = 0) -> dict:
    keys = jax.random.split(jax.random.key(seed), 7)
    image_emb = centred(keys[0], (TOKENS, D), (D ** -0.5), 0.17675781, ((0, 768),))
    text_emb = centred(keys[1], (TOKENS, D), (D ** -0.5), 0.17677669, ((0, 768),), jnp.float32)
    text_accum = centred(keys[2], (TOKENS, D), 1.0, 6.0, ((0, 768),), jnp.float32)
    pair_ids = set_ends(jax.random.randint(keys[3], (TOKENS,), 0, TOK_DEV // 2), jax.random.fold_in(keys[3], 1), 0, (TOK_DEV // 2) - 1).astype(jnp.int32)
    log_scale = jnp.clip(jax.random.uniform(keys[4], (1,), jnp.float32, 1.0, 2.0), 1.0, 2.0)
    bias = jnp.clip(jax.random.uniform(keys[5], (1,), jnp.float32, -3.0, 0.0), -3.0, 0.0)
    return {"image_emb": image_emb, "text_emb": text_emb, "text_accum": text_accum, "pair_ids": pair_ids, "log_scale": log_scale, "bias": bias}


def block_terms(image_block, text_block, image_ids, text_ids, scale, shift):
    logits = scale * lax.dot_general(image_block, text_block, (((1,), (1,)), ((), ())), preferred_element_type=jnp.float32) + shift
    signs = jnp.where(image_ids[:, None] == text_ids[None, :], 1.0, -1.0).astype(jnp.float32)
    loss = jnp.sum(jax.nn.softplus(-signs * logits), axis=1)
    coef = (-signs * jax.nn.sigmoid(-signs * logits) * scale).astype(jnp.bfloat16)
    image_part = jnp.dot(coef, text_block, preferred_element_type=jnp.float32)
    text_part = lax.dot_general(coef, image_block, (((0,), (0,)), ((), ())), preferred_element_type=jnp.float32)
    return loss, image_part, text_part


def reference(image_emb, text_emb, text_accum, pair_ids, log_scale, bias):
    blocks = TOKENS // TOK_DEV
    scale = jnp.exp(log_scale[0])
    shift = bias[0]
    text_low = text_emb.astype(jnp.bfloat16)
    images = image_emb.reshape(blocks, TOK_DEV, D)
    texts = text_low.reshape(blocks, TOK_DEV, D)
    id_rows = pair_ids.reshape(blocks, TOK_DEV)

    def one_block(index):
        image_block = images[index]
        image_ids = id_rows[index]
        loss = jnp.zeros((TOK_DEV,), jnp.float32)
        image_sum = jnp.zeros((TOK_DEV, D), jnp.float32)
        text_parts = []
        for step in range(SHIFTS + 1):
            other = (index - step) % blocks
            part_loss, image_part, text_part = block_terms(image_block, texts[other], image_ids, id_rows[other], scale, shift)
            loss = loss + part_loss
            image_sum = image_sum + image_part
            text_parts.append(text_part)
        return loss, image_sum.astype(jnp.bfloat16), jnp.stack(text_parts)

    losses, image_grads, text_parts = lax.map(one_block, jnp.arange(blocks, dtype=jnp.int32))
    row_loss = (losses / ((SHIFTS + 1) * TOK_DEV)).reshape(TOKENS)
    total = text_accum.reshape(blocks, TOK_DEV, D)
    for step in range(SHIFTS + 1):
        total = total + jnp.roll(text_parts[:, step], -step, axis=0)
    text_grad = jnp.roll(total, SHIFTS, axis=0).reshape(TOKENS, D)
    return row_loss, image_grads.reshape(TOKENS, D), text_grad
```

```python
import functools

import jax
import jax.numpy as jnp
from jax import lax
from jax.experimental import pallas as pl
from jax.experimental.pallas import tpu as pltpu
from jax.sharding import PartitionSpec as P

SHIFTS = 2
Y = 8
TILE = 384
MESH = pl.DeviceIdType.MESH

AHEAD_T = [(64 + 32 * i, 32) for i in range(6)]
BACK_T = [(16 * i, 16) for i in range(4)]
AHEAD_C = [(64 + 32 * i, 32) for i in range(5)] + [(224, 16), (240, 16)]
BACK_C = [(16 * i, 16) for i in range(4)]


def places(zs, dps):
    dp = lax.axis_index("dp")
    group = lax.axis_index("group")
    core = group % 2
    y_hi = group // 2
    z = dp % zs
    y_lo = (dp // zs) % 2
    x = dp // (2 * zs)
    y = y_hi * 2 + y_lo

    def chip(x, y, z):
        return ((x * 2 + y % 2) * zs + z, (y // 2) * 2 + core)

    def after(place):
        dp, group = place
        return ((dp + group // 6) % dps, (group + 2) % 8)

    def before(place):
        dp, group = place
        return ((dp + dps - (7 - group) // 6) % dps, (group + 6) % 8)

    me = (dp, group)
    mate = (dp, group + 1 - 2 * core)
    via = chip(x, (y + Y - 3) % Y, z)
    source = chip(x, (y + 3) % Y, z)
    previous = before(me)
    p_dp, p_group = previous
    p_y = (p_group // 2) * 2 + (p_dp // zs) % 2
    p_via = chip(p_dp // (2 * zs), (p_y + Y - 3) % Y, p_dp % zs)
    return dict(
        core=core,
        mate=mate,
        after=after(me),
        previous=previous,
        via=via,
        source=source,
        onward=after(source),
        previous_via=p_via,
    )


def kernel(
    zs,
    dps,
    log_scale,
    bias,
    image_hbm,
    text_hbm,
    accum_hbm,
    ids_hbm,
    loss_hbm,
    image_grad_hbm,
    text_grad_hbm,
    image,
    text,
    accum,
    own,
    mate_text,
    far_text,
    coef,
    grad,
    part,
    mate_part,
    total,
    carried,
    far_carried,
    passing,
    loss,
    loss_row,
    image_grad,
    ids,
    mate_ids,
    far_ids,
    load_sem,
    store_sem,
    sends,
    recvs,
):
    at = places(zs, dps)
    core = at["core"]
    is0 = core == 0
    is1 = core == 1
    barrier = pltpu.get_barrier_semaphore()
    for name in ("mate", "previous", "source", "previous_via"):
        pl.semaphore_signal(barrier, inc=1, device_id=at[name], device_id_type=MESH)

    loads = [
        pltpu.make_async_copy(src, dst, load_sem.at[i])
        for i, (src, dst) in enumerate(
            [(text_hbm, text), (image_hbm, image), (ids_hbm, ids), (accum_hbm, accum)]
        )
    ]
    for copy in loads:
        copy.start()

    count = [0]

    def remote(src, dst, to):
        k = count[0]
        count[0] += 1
        return pltpu.make_async_remote_copy(
            src_ref=src,
            dst_ref=dst,
            send_sem=sends.at[k],
            recv_sem=recvs.at[k],
            device_id=at[to],
            device_id_type=MESH,
        )

    def rows(ref, piece, shift=0):
        return ref.at[pl.ds(piece[0] + shift, piece[1])]

    back_t = sum(n for _, n in BACK_T)
    text_ahead = [remote(rows(own, p), rows(far_text, p), "after") for p in AHEAD_T]
    text_leg1 = [remote(rows(own, p), rows(passing, p), "via") for p in BACK_T]
    text_leg2 = [remote(rows(passing, p), rows(far_text, p), "onward") for p in BACK_T]
    carry_ahead = [remote(rows(carried, p), rows(far_carried, p), "after") for p in AHEAD_C]
    carry_leg1 = [remote(rows(carried, p), rows(passing, p, back_t), "via") for p in BACK_C]
    carry_leg2 = [remote(rows(passing, p, back_t), rows(far_carried, p), "onward") for p in BACK_C]
    ids_ahead = remote(ids, far_ids, "after")
    text_down = remote(own, mate_text, "mate")
    ids_down = remote(ids, mate_ids, "mate")
    far_pieces = BACK_T + AHEAD_T
    text_up = [remote(rows(far_text, p), rows(mate_text, p), "mate") for p in far_pieces]
    ids_up = remote(far_ids, mate_ids, "mate")
    part_over = remote(part, mate_part, "mate")

    scale = jnp.exp(jnp.full((1, 256), log_scale[0], jnp.float32))
    shift = bias[0]

    def terms(text_block, text_ids, first, out):
        image_ids = jnp.transpose(jnp.broadcast_to(ids[...].astype(jnp.float32), (128, 256)))
        other = text_ids[...].astype(jnp.float32)
        for i in range(2):
            at_rows = pl.ds(128 * i, 128)
            logits = (
                scale
                * lax.dot_general(
                    image[at_rows, :],
                    text_block[...],
                    (((1,), (1,)), ((), ())),
                    preferred_element_type=jnp.float32,
                )
                + shift
            )
            mine = image_ids[128 * i : 128 * (i + 1), 0:1]
            minus = jnp.where(mine == other, -1.0, 1.0)
            u = minus * logits
            e = jnp.exp(-jnp.abs(u))
            soft = jnp.maximum(u, 0.0) + jnp.log1p(e)
            sig = jnp.where(u >= 0, 1.0, e) / (1.0 + e)
            coef[at_rows, :] = (minus * sig * scale).astype(jnp.bfloat16)
            folded = soft[:, :128] + soft[:, 128:]
            if first:
                loss[at_rows, :] = folded
            else:
                loss[at_rows, :] = loss[at_rows, :] + folded
        for j in range(image.shape[1] // TILE):
            cols = pl.ds(TILE * j, TILE)
            g = jnp.dot(coef[...], text_block[:, cols], preferred_element_type=jnp.float32)
            if first:
                grad[:, cols] = g
            else:
                grad[:, cols] = grad[:, cols] + g
            out[:, cols] = lax.dot_general(
                coef[...],
                image[:, cols],
                (((0,), (0,)), ((), ())),
                preferred_element_type=jnp.float32,
            )

    loads[0].wait()
    own[...] = text[...].astype(jnp.bfloat16)
    loads[1].wait()
    loads[2].wait()
    pl.semaphore_wait(barrier, 4)

    for i in range(max(len(text_leg1), len(text_ahead))):
        if i < len(text_leg1):
            text_leg1[i].start()
        if i < len(text_ahead):
            text_ahead[i].start()
        if i == 0:
            ids_ahead.start()

            @pl.when(is0)
            def _():
                text_down.start()
                ids_down.start()

    terms(own, ids, True, total)
    loads[3].wait()

    @pl.when(is1)
    def _():
        carried[...] = (total[...] + accum[...]).astype(jnp.bfloat16)
        text_down.wait_recv()
        ids_down.wait_recv()
        terms(mate_text, mate_ids, False, part)
        part_over.start()

    @pl.when(is0)
    def _():
        part_over.wait_recv()
        carried[...] = (total[...] + accum[...] + mate_part[...]).astype(jnp.bfloat16)

    for copy in carry_ahead:
        copy.start()
    for i in range(max(len(text_leg1), len(carry_leg1))):
        if i < len(text_leg1):
            text_leg1[i].wait_recv()
            text_leg2[i].start()
        if i < len(carry_leg1):
            carry_leg1[i].start()

    ids_ahead.wait_recv()

    @pl.when(is1)
    def _():
        ids_up.start()

    order = list(range(len(BACK_T), len(far_pieces))) + list(range(len(BACK_T)))
    for i in order:
        (text_leg2[i] if i < len(BACK_T) else text_ahead[i - len(BACK_T)]).wait_recv()

        @pl.when(is1)
        def _():
            text_up[i].start()

    @pl.when(is0)
    def _():
        ids_up.wait_recv()
        for i in order:
            text_up[i].wait_recv()
        terms(mate_text, mate_ids, False, part)
        part_over.start()

    terms(far_text, far_ids, False, total)

    image_grad[...] = grad[...].astype(jnp.bfloat16)
    store_image = pltpu.make_async_copy(image_grad, image_grad_hbm, store_sem.at[0])
    store_image.start()
    columns = (SHIFTS + 1) * image.shape[0]
    loss_row[...] = jnp.sum(jnp.transpose(loss[...]), axis=0, keepdims=True) / columns
    store_loss = pltpu.make_async_copy(loss_row, loss_hbm, store_sem.at[1])
    store_loss.start()

    @pl.when(is1)
    def _():
        part_over.wait_recv()
        total[...] = total[...] + mate_part[...]

    stores = []

    def finish(copy, piece):
        copy.wait_recv()
        at_rows = pl.ds(piece[0], piece[1])
        total[at_rows, :] = total[at_rows, :] + far_carried[at_rows, :].astype(jnp.float32)
        store = pltpu.make_async_copy(
            rows(total, piece), rows(text_grad_hbm, piece), store_sem.at[2 + len(stores)]
        )
        store.start()
        stores.append(store)

    half = len(carry_ahead) // 2
    for i in range(half):
        finish(carry_ahead[i], AHEAD_C[i])
    for i in range(len(carry_leg1)):
        carry_leg1[i].wait_recv()
        carry_leg2[i].start()
    for i in range(max(len(carry_ahead) - half, len(carry_leg2))):
        if half + i < len(carry_ahead):
            finish(carry_ahead[half + i], AHEAD_C[half + i])
        if i < len(carry_leg2):
            finish(carry_leg2[i], BACK_C[i])

    for group in (text_ahead, text_leg1, text_leg2, carry_ahead, carry_leg1, carry_leg2):
        for copy in group:
            copy.wait_send()
    ids_ahead.wait_send()
    part_over.wait_send()

    @pl.when(is0)
    def _():
        text_down.wait_send()
        ids_down.wait_send()

    @pl.when(is1)
    def _():
        ids_up.wait_send()
        for copy in text_up:
            copy.wait_send()

    store_image.wait()
    store_loss.wait()
    for store in stores:
        store.wait()


def solution(mesh):
    dps = mesh.shape["dp"]
    zs = dps // 8 if dps >= 8 else 1
    copies = 3 * len(BACK_T) + 2 * len(AHEAD_T) + len(AHEAD_C) + 2 * len(BACK_C) + 5
    pieces = len(AHEAD_C) + len(BACK_C)
    passing_rows = sum(n for _, n in BACK_T) + sum(n for _, n in BACK_C)

    def body(image_emb, text_emb, text_accum, pair_ids, log_scale, bias):
        n, d = image_emb.shape
        any_space = pl.BlockSpec(memory_space=pl.ANY)
        scalar = pl.BlockSpec(memory_space=pltpu.SMEM)
        f32, bf16, i32 = jnp.float32, jnp.bfloat16, jnp.int32
        loss, image_grad, text_grad = pl.pallas_call(
            functools.partial(kernel, zs, dps),
            out_shape=(
                jax.ShapeDtypeStruct((1, n), f32),
                jax.ShapeDtypeStruct((n, d), bf16),
                jax.ShapeDtypeStruct((n, d), f32),
            ),
            in_specs=[scalar, scalar, any_space, any_space, any_space, any_space],
            out_specs=(any_space, any_space, any_space),
            scratch_shapes=[
                pltpu.VMEM((n, d), bf16),
                pltpu.VMEM((n, d), f32),
                pltpu.VMEM((n, d), f32),
                pltpu.VMEM((n, d), bf16),
                pltpu.VMEM((n, d), bf16),
                pltpu.VMEM((n, d), bf16),
                pltpu.VMEM((n, n), bf16),
                pltpu.VMEM((n, d), f32),
                pltpu.VMEM((n, d), f32),
                pltpu.VMEM((n, d), f32),
                pltpu.VMEM((n, d), f32),
                pltpu.VMEM((n, d), bf16),
                pltpu.VMEM((n, d), bf16),
                pltpu.VMEM((passing_rows, d), bf16),
                pltpu.VMEM((n, 128), f32),
                pltpu.VMEM((1, n), f32),
                pltpu.VMEM((n, d), bf16),
                pltpu.VMEM((1, n), i32),
                pltpu.VMEM((1, n), i32),
                pltpu.VMEM((1, n), i32),
                pltpu.SemaphoreType.DMA((4,)),
                pltpu.SemaphoreType.DMA((2 + pieces,)),
                pltpu.SemaphoreType.DMA((copies,)),
                pltpu.SemaphoreType.DMA((copies,)),
            ],
            compiler_params=pltpu.CompilerParams(
                collective_id=0, has_side_effects=True, vmem_limit_bytes=40 << 20
            ),
        )(log_scale, bias, image_emb, text_emb, text_accum, pair_ids.reshape(1, n))
        return loss.reshape(n), image_grad, text_grad

    split = P(("dp", "group"))
    wide = P(("dp", "group"), None)
    return jax.shard_map(
        body,
        mesh=mesh,
        in_specs=(wide, wide, wide, split, P(), P()),
        out_specs=(split, wide, wide),
        check_vma=False,
    )
```

```python
import functools

import jax
import jax.numpy as jnp
from jax import lax
from jax.experimental import pallas as pl
from jax.experimental.pallas import tpu as pltpu
from jax.sharding import PartitionSpec as P

SHIFTS = 2
Y = 8
TILE = 384
MESH = pl.DeviceIdType.MESH

AHEAD_T = [(64 + 32 * i, 32) for i in range(6)]
BACK_T = [(16 * i, 16) for i in range(4)]
AHEAD_C = [(64 + 32 * i, 32) for i in range(5)] + [(224, 16), (240, 16)]
BACK_C = [(16 * i, 16) for i in range(4)]
SWING_T = [2, 3]
SWING_C = [2, 3]


def places(zs, dps):
    dp = lax.axis_index("dp")
    group = lax.axis_index("group")
    core = group % 2
    y_hi = group // 2
    z = dp % zs
    y_lo = (dp // zs) % 2
    x = dp // (2 * zs)
    y = y_hi * 2 + y_lo

    def chip(x, y, z):
        return ((x * 2 + y % 2) * zs + z, (y // 2) * 2 + core)

    def after(place):
        dp, group = place
        return ((dp + group // 6) % dps, (group + 2) % 8)

    def before(place):
        dp, group = place
        return ((dp + dps - (7 - group) // 6) % dps, (group + 6) % 8)

    me = (dp, group)
    mate = (dp, group + 1 - 2 * core)
    via = chip(x, (y + Y - 3) % Y, z)
    source = chip(x, (y + 3) % Y, z)
    previous = before(me)
    p_dp, p_group = previous
    p_y = (p_group // 2) * 2 + (p_dp // zs) % 2
    p_via = chip(p_dp // (2 * zs), (p_y + Y - 3) % Y, p_dp % zs)
    last = z == zs - 1
    return dict(
        core=core,
        long=last & (y == 6),
        long_relay=last & (y == 3),
        short=last & (y == 7),
        short_relay=last & (y == 4),
        mate=mate,
        after=after(me),
        previous=previous,
        via=via,
        source=source,
        onward=after(source),
        previous_via=p_via,
    )


def kernel(
    zs,
    dps,
    log_scale_hbm,
    bias_hbm,
    image_hbm,
    text_hbm,
    accum_hbm,
    ids_hbm,
    loss_hbm,
    image_grad_hbm,
    text_grad_hbm,
    image,
    text,
    accum,
    own,
    mate_text,
    far_text,
    coef,
    grad,
    part,
    mate_part,
    total,
    carried,
    far_carried,
    passing,
    loss,
    loss_row,
    image_grad,
    ids,
    mate_ids,
    far_ids,
    log_scale,
    bias,
    load_sem,
    store_sem,
    sends,
    recvs,
):
    at = places(zs, dps)
    core = at["core"]
    is0 = core == 0
    is1 = core == 1
    barrier = pltpu.get_barrier_semaphore()
    for name in ("mate", "previous", "source", "previous_via"):
        pl.semaphore_signal(barrier, inc=1, device_id=at[name], device_id_type=MESH)

    loads = [
        pltpu.make_async_copy(src, dst, load_sem.at[i])
        for i, (src, dst) in enumerate(
            [
                (text_hbm, text),
                (image_hbm, image),
                (ids_hbm, ids),
                (log_scale_hbm, log_scale),
                (bias_hbm, bias),
                (accum_hbm, accum),
            ]
        )
    ]
    for copy in loads:
        copy.start()

    count = [0]

    def fresh():
        count[0] += 1
        return count[0] - 1

    def remote(src, dst, to, send=None, recv=None):
        k = fresh() if send is None or recv is None else 0
        return pltpu.make_async_remote_copy(
            src_ref=src,
            dst_ref=dst,
            send_sem=sends.at[k if send is None else send],
            recv_sem=recvs.at[k if recv is None else recv],
            device_id=at[to],
            device_id_type=MESH,
        )

    def rows(ref, piece, shift=0):
        return ref.at[pl.ds(piece[0] + shift, piece[1])]

    short, short_relay = at["short"], at["short_relay"]
    long, long_relay = at["long"], at["long_relay"]
    room = [0]

    class Stream:
        def __init__(self, src, dst, ahead, back, swing):
            self.ahead, self.back, self.swing = ahead, back, swing
            ahead_ids = [fresh() for _ in ahead]
            leg1_ids = [fresh() for _ in back]
            leg2_ids = [fresh() for _ in back]
            swing_ids = [fresh() for _ in swing]

            def hop(src, dst, to, send, recv):
                return remote(src, dst, to, send, recv)

            def slot(piece):
                room[0] += piece[1]
                return passing.at[pl.ds(room[0] - piece[1], piece[1])]

            slots = [slot(p) for p in back]
            swing_slots = [slot(ahead[i]) for i in swing]
            self.straight = [
                hop(rows(src, p), rows(dst, p), "after", k, k) for p, k in zip(ahead, ahead_ids)
            ]
            self.leg1 = [
                hop(rows(src, p), t, "via", k, k) for p, t, k in zip(back, slots, leg1_ids)
            ]
            self.leg2 = [
                hop(t, rows(dst, p), "onward", k, k) for p, t, k in zip(back, slots, leg2_ids)
            ]
            self.instead = [
                hop(rows(src, p), rows(dst, p), "after", k1, k2)
                for p, k1, k2 in zip(back, leg1_ids, leg2_ids)
            ]
            self.swing1 = [
                hop(rows(src, ahead[i]), t, "via", ahead_ids[i], k)
                for i, t, k in zip(swing, swing_slots, swing_ids)
            ]
            self.swing2 = [
                hop(t, rows(dst, ahead[i]), "onward", k, ahead_ids[i])
                for i, t, k in zip(swing, swing_slots, swing_ids)
            ]

        def send_ahead(self, i):
            if i in self.swing:

                @pl.when(long)
                def _():
                    self.swing1[self.swing.index(i)].start()

                @pl.when(jnp.logical_not(long))
                def _():
                    self.straight[i].start()

            else:
                self.straight[i].start()

        def send_back(self, i):
            @pl.when(short)
            def _():
                self.instead[i].start()

            @pl.when(jnp.logical_not(short))
            def _():
                self.leg1[i].start()

        def relay(self, i):
            @pl.when(jnp.logical_not(short_relay))
            def _():
                self.leg1[i].wait_recv()
                self.leg2[i].start()

        def relay_swing(self):
            @pl.when(long_relay)
            def _():
                for one, two in zip(self.swing1, self.swing2):
                    one.wait_recv()
                    two.start()

        def wait_sends(self):
            for copy in self.straight + self.leg1:
                copy.wait_send()

            @pl.when(jnp.logical_not(short_relay))
            def _():
                for copy in self.leg2:
                    copy.wait_send()

            @pl.when(long_relay)
            def _():
                for copy in self.swing2:
                    copy.wait_send()

    texts = Stream(own, far_text, AHEAD_T, BACK_T, SWING_T)
    carries = Stream(carried, far_carried, AHEAD_C, BACK_C, SWING_C)
    ids_ahead = remote(ids, far_ids, "after")
    text_down = remote(own, mate_text, "mate")
    ids_down = remote(ids, mate_ids, "mate")
    arrivals = [(texts.straight[i], AHEAD_T[i]) for i in range(len(AHEAD_T)) if i not in SWING_T]
    arrivals += [(texts.leg2[i], BACK_T[i]) for i in range(len(BACK_T))]
    arrivals += [(texts.straight[i], AHEAD_T[i]) for i in SWING_T]
    text_up = [remote(rows(far_text, p), rows(mate_text, p), "mate") for _, p in arrivals]
    ids_up = remote(far_ids, mate_ids, "mate")
    part_over = remote(part, mate_part, "mate")

    def terms(text_block, text_ids, first, out):
        scale = jnp.exp(jnp.full((1, 256), log_scale[0], jnp.float32))
        shift = bias[0]
        image_ids = jnp.transpose(jnp.broadcast_to(ids[...].astype(jnp.float32), (128, 256)))
        other = text_ids[...].astype(jnp.float32)
        for i in range(2):
            at_rows = pl.ds(128 * i, 128)
            logits = (
                scale
                * lax.dot_general(
                    image[at_rows, :],
                    text_block[...],
                    (((1,), (1,)), ((), ())),
                    preferred_element_type=jnp.float32,
                )
                + shift
            )
            mine = image_ids[128 * i : 128 * (i + 1), 0:1]
            minus = jnp.where(mine == other, -1.0, 1.0)
            u = minus * logits
            e = jnp.exp(-jnp.abs(u))
            soft = jnp.maximum(u, 0.0) + jnp.log1p(e)
            sig = jnp.where(u >= 0, 1.0, e) / (1.0 + e)
            coef[at_rows, :] = (minus * sig * scale).astype(jnp.bfloat16)
            folded = soft[:, :128] + soft[:, 128:]
            if first:
                loss[at_rows, :] = folded
            else:
                loss[at_rows, :] = loss[at_rows, :] + folded
        for j in range(image.shape[1] // TILE):
            cols = pl.ds(TILE * j, TILE)
            g = jnp.dot(coef[...], text_block[:, cols], preferred_element_type=jnp.float32)
            if first:
                grad[:, cols] = g
            else:
                grad[:, cols] = grad[:, cols] + g
            out[:, cols] = lax.dot_general(
                coef[...],
                image[:, cols],
                (((0,), (0,)), ((), ())),
                preferred_element_type=jnp.float32,
            )

    loads[0].wait()
    own[...] = text[...].astype(jnp.bfloat16)
    for copy in loads[1:5]:
        copy.wait()
    terms(own, ids, True, total)
    loads[5].wait()

    @pl.when(is1)
    def _():
        carried[...] = (total[...] + accum[...]).astype(jnp.bfloat16)

    pl.semaphore_wait(barrier, 4)

    for i in range(max(len(BACK_T), len(AHEAD_T))):
        if i < len(BACK_T):
            texts.send_back(i)
        if i < len(AHEAD_T):
            texts.send_ahead(i)
        if i == 0:
            ids_ahead.start()

            @pl.when(is0)
            def _():
                text_down.start()
                ids_down.start()

    @pl.when(is1)
    def _():
        text_down.wait_recv()
        ids_down.wait_recv()
        terms(mate_text, mate_ids, False, part)
        part_over.start()

    @pl.when(is0)
    def _():
        part_over.wait_recv()
        carried[...] = (total[...] + accum[...] + mate_part[...]).astype(jnp.bfloat16)

    for i in range(len(AHEAD_C)):
        carries.send_ahead(i)
    for i in range(max(len(BACK_T), len(BACK_C))):
        if i < len(BACK_T):
            texts.relay(i)
        if i < len(BACK_C):
            carries.send_back(i)
    texts.relay_swing()

    ids_ahead.wait_recv()

    @pl.when(is1)
    def _():
        ids_up.start()

    for i, (copy, _) in enumerate(arrivals):
        copy.wait_recv()

        @pl.when(is1)
        def _():
            text_up[i].start()

    early = len(BACK_C) // 2
    for i in range(early):
        carries.relay(i)

    @pl.when(is0)
    def _():
        ids_up.wait_recv()
        for copy in text_up:
            copy.wait_recv()
        terms(mate_text, mate_ids, False, part)
        part_over.start()

    for i in range(early, len(BACK_C)):
        carries.relay(i)
    carries.relay_swing()

    terms(far_text, far_ids, False, total)

    image_grad[...] = grad[...].astype(jnp.bfloat16)
    store_image = pltpu.make_async_copy(image_grad, image_grad_hbm, store_sem.at[0])
    store_image.start()
    columns = (SHIFTS + 1) * image.shape[0]
    loss_row[...] = jnp.sum(jnp.transpose(loss[...]), axis=0, keepdims=True) / columns
    store_loss = pltpu.make_async_copy(loss_row, loss_hbm, store_sem.at[1])
    store_loss.start()

    @pl.when(is1)
    def _():
        part_over.wait_recv()
        total[...] = total[...] + mate_part[...]

    stores = []

    def finish(copy, piece):
        copy.wait_recv()
        at_rows = pl.ds(piece[0], piece[1])
        total[at_rows, :] = total[at_rows, :] + far_carried[at_rows, :].astype(jnp.float32)
        store = pltpu.make_async_copy(
            rows(total, piece), rows(text_grad_hbm, piece), store_sem.at[2 + len(stores)]
        )
        store.start()
        stores.append(store)

    half = len(AHEAD_C) - len(BACK_C)
    for i in range(half):
        finish(carries.straight[i], AHEAD_C[i])
    for i in range(len(BACK_C)):
        finish(carries.leg2[i], BACK_C[i])
        finish(carries.straight[half + i], AHEAD_C[half + i])

    texts.wait_sends()
    carries.wait_sends()
    ids_ahead.wait_send()
    part_over.wait_send()

    @pl.when(is0)
    def _():
        text_down.wait_send()
        ids_down.wait_send()

    @pl.when(is1)
    def _():
        ids_up.wait_send()
        for copy in text_up:
            copy.wait_send()

    store_image.wait()
    store_loss.wait()
    for store in stores:
        store.wait()


def store_kernel(loss, image_grad, text_grad, loss_hbm, image_grad_hbm, text_grad_hbm, sem):
    copies = [
        pltpu.make_async_copy(src, dst, sem.at[i])
        for i, (src, dst) in enumerate(
            [(text_grad, text_grad_hbm), (image_grad, image_grad_hbm), (loss, loss_hbm)]
        )
    ]
    for copy in copies:
        copy.start()
    for copy in copies:
        copy.wait()


def solution(mesh):
    dps = mesh.shape["dp"]
    zs = dps // 8 if dps >= 8 else 1
    copies = 3 * len(BACK_T) + 2 * len(AHEAD_T) + len(AHEAD_C) + 2 * len(BACK_C) + 5
    copies += len(SWING_T) + len(SWING_C)
    pieces = len(AHEAD_C) + len(BACK_C)
    passing_rows = sum(n for _, n in BACK_T) + sum(n for _, n in BACK_C)
    passing_rows += sum(AHEAD_T[i][1] for i in SWING_T) + sum(AHEAD_C[i][1] for i in SWING_C)

    def body(image_emb, text_emb, text_accum, pair_ids, log_scale, bias):
        n, d = image_emb.shape
        any_space = pl.BlockSpec(memory_space=pl.ANY)
        hbm = pl.BlockSpec(memory_space=pltpu.HBM)
        f32, bf16, i32 = jnp.float32, jnp.bfloat16, jnp.int32
        shapes = (
            jax.ShapeDtypeStruct((1, n), f32),
            jax.ShapeDtypeStruct((n, d), bf16),
            jax.ShapeDtypeStruct((n, d), f32),
        )
        results = pl.pallas_call(
            functools.partial(kernel, zs, dps),
            out_shape=shapes,
            in_specs=[hbm] * 6,
            out_specs=(any_space, any_space, any_space),
            scratch_shapes=[
                pltpu.VMEM((n, d), bf16),
                pltpu.VMEM((n, d), f32),
                pltpu.VMEM((n, d), f32),
                pltpu.VMEM((n, d), bf16),
                pltpu.VMEM((n, d), bf16),
                pltpu.VMEM((n, d), bf16),
                pltpu.VMEM((n, n), bf16),
                pltpu.VMEM((n, d), f32),
                pltpu.VMEM((n, d), f32),
                pltpu.VMEM((n, d), f32),
                pltpu.VMEM((n, d), f32),
                pltpu.VMEM((n, d), bf16),
                pltpu.VMEM((n, d), bf16),
                pltpu.VMEM((passing_rows, d), bf16),
                pltpu.VMEM((n, 128), f32),
                pltpu.VMEM((1, n), f32),
                pltpu.VMEM((n, d), bf16),
                pltpu.VMEM((1, n), i32),
                pltpu.VMEM((1, n), i32),
                pltpu.VMEM((1, n), i32),
                pltpu.SMEM((1,), f32),
                pltpu.SMEM((1,), f32),
                pltpu.SemaphoreType.DMA((6,)),
                pltpu.SemaphoreType.DMA((2 + pieces,)),
                pltpu.SemaphoreType.DMA((copies,)),
                pltpu.SemaphoreType.DMA((copies,)),
            ],
            compiler_params=pltpu.CompilerParams(
                collective_id=0, has_side_effects=True, vmem_limit_bytes=51 << 20
            ),
        )(log_scale, bias, image_emb, text_emb, text_accum, pair_ids.reshape(1, n))
        loss, image_grad, text_grad = pl.pallas_call(
            store_kernel,
            out_shape=shapes,
            in_specs=[any_space] * 3,
            out_specs=(hbm, hbm, hbm),
            scratch_shapes=[pltpu.SemaphoreType.DMA((3,))],
            compiler_params=pltpu.CompilerParams(vmem_limit_bytes=1 << 20),
        )(*results)
        return loss.reshape(n), image_grad, text_grad

    split = P(("dp", "group"))
    wide = P(("dp", "group"), None)
    return jax.shard_map(
        body,
        mesh=mesh,
        in_specs=(wide, wide, wide, split, P(), P()),
        out_specs=(split, wide, wide),
        check_vma=False,
    )
```

```python
import functools

import jax
import jax.numpy as jnp
from jax import lax
from jax.experimental import pallas as pl
from jax.experimental.pallas import tpu as pltpu
from jax.sharding import PartitionSpec as P

SHIFTS = 2
Y = 8
TILE = 384
MESH = pl.DeviceIdType.MESH

AHEAD_T = [(64 + 32 * i, 32) for i in range(6)]
BACK_T = [(16 * i, 16) for i in range(4)]
AHEAD_C = [(64 + 32 * i, 32) for i in range(5)] + [(224, 16), (240, 16)]
BACK_C = [(16 * i, 16) for i in range(4)]
HELP_T = {12: (1, 2, 3, 4, 5, 6, 7, 8, 9, 10)}
HELP_C = {12: (1, 2, 3, 4)}


def places(zs, dps):
    dp = lax.axis_index("dp")
    group = lax.axis_index("group")
    xs = max(dps // (2 * zs), 1)
    core = group % 2
    z = dp % zs
    y = (group // 2) * 2 + (dp // zs) % 2
    x = dp // (2 * zs)
    last = z == zs - 1
    helpers = HELP_T.get(zs, ())

    def chip(x, y, z):
        return ((x * 2 + y % 2) * zs + z, (y // 2) * 2 + core)

    def after(place):
        dp, group = place
        return ((dp + group // 6) % dps, (group + 2) % 8)

    def relay(x, y, z):
        turn = jnp.where((z == zs - 1) & (y == 6), 1, 0)
        return chip(x, (y + Y - 3 + turn) % Y, z)

    source = chip(x, (y + 3 - jnp.where(last & (y == 4), 1, 0)) % Y, z)
    previous = ((dp + dps - (7 - group) // 6) % dps, (group + 6) % 8)
    p_dp, p_group = previous
    p_z = p_dp % zs
    p_y = (p_group // 2) * 2 + (p_dp // zs) % 2
    helper = z < 0
    for z_j in helpers:
        helper = helper | ((y == 0) & (z == z_j))
    return dict(
        core=core,
        z=z,
        short=last & (y == 7),
        idle=last & (y == 3),
        end=(p_z == zs - 1) & (p_y == 7),
        late=(p_z == zs - 1) & (p_y >= 6),
        helper=helper,
        mate=(dp, group + 1 - 2 * core),
        after=after((dp, group)),
        previous=previous,
        via=relay(x, y, z),
        source=source,
        onward=after(source),
        previous_via=relay(p_dp // (2 * zs), p_y, p_z),
        helped=chip(x, 7, zs - 1),
        help_end=chip((x + 1) % xs, 0, 0),
        helpers=[chip(x, 0, z_j) for z_j in helpers],
        end_helpers=[chip((x + xs - 1) % xs, 0, z_j) for z_j in helpers],
    )


def kernel(
    zs,
    dps,
    log_scale_hbm,
    bias_hbm,
    image_hbm,
    text_hbm,
    accum_hbm,
    ids_hbm,
    loss_hbm,
    image_grad_hbm,
    text_grad_hbm,
    image,
    text,
    accum,
    own,
    mate_text,
    far_text,
    coef,
    grad,
    part,
    mate_part,
    total,
    carried,
    far_carried,
    passing,
    loss,
    loss_row,
    image_grad,
    ids,
    mate_ids,
    far_ids,
    log_scale,
    bias,
    load_sem,
    store_sem,
    sends,
    recvs,
):
    at = places(zs, dps)
    core = at["core"]
    is0 = core == 0
    is1 = core == 1
    short, idle, end, helper = at["short"], at["idle"], at["end"], at["helper"]
    helpers = HELP_T.get(zs, ())
    barrier = pltpu.get_barrier_semaphore()

    def greet(place):
        pl.semaphore_signal(barrier, inc=1, device_id=place, device_id_type=MESH)

    greet(at["mate"])
    greet(at["previous"])

    @pl.when(jnp.logical_not(idle))
    def _():
        greet(at["source"])

    @pl.when(jnp.logical_not(end))
    def _():
        greet(at["previous_via"])

    if helpers:

        @pl.when(end)
        def _():
            for place in at["end_helpers"]:
                greet(place)

        @pl.when(helper)
        def _():
            greet(at["helped"])

    partners = 2 + jnp.where(short, len(helpers), 1) + jnp.where(idle, 0, 1) + jnp.where(helper, 1, 0)

    loads = [
        pltpu.make_async_copy(src, dst, load_sem.at[i])
        for i, (src, dst) in enumerate(
            [
                (text_hbm, text),
                (image_hbm, image),
                (ids_hbm, ids),
                (log_scale_hbm, log_scale),
                (bias_hbm, bias),
                (accum_hbm, accum),
            ]
        )
    ]
    for copy in loads:
        copy.start()

    count = [0]

    def fresh():
        count[0] += 1
        return count[0] - 1

    def remote(src, dst, to, send=None, recv=None):
        k = fresh() if send is None or recv is None else 0
        return pltpu.make_async_remote_copy(
            src_ref=src,
            dst_ref=dst,
            send_sem=sends.at[k if send is None else send],
            recv_sem=recvs.at[k if recv is None else recv],
            device_id=at[to] if isinstance(to, str) else to,
            device_id_type=MESH,
        )

    def rows(ref, piece, shift=0):
        return ref.at[pl.ds(piece[0] + shift, piece[1])]

    room = [0]

    def slot(n):
        room[0] += n
        return passing.at[pl.ds(room[0] - n, n)]

    class Stream:
        def __init__(self, src, dst, ahead, back, help_z):
            self.ahead, self.back = ahead, back
            ahead_ids = [fresh() for _ in ahead]
            leg1_ids = [fresh() for _ in back]
            leg2_ids = [fresh() for _ in back]
            self.straight = [
                remote(rows(src, p), rows(dst, p), "after", k, k) for p, k in zip(ahead, ahead_ids)
            ]
            slots = [slot(n) for _, n in back]
            self.leg1 = [
                remote(rows(src, p), t, "via", k, k) for p, t, k in zip(back, slots, leg1_ids)
            ]
            self.leg2 = [
                remote(t, rows(dst, p), "onward", k, k) for p, t, k in zip(back, slots, leg2_ids)
            ]
            self.instead = [
                remote(rows(src, p), rows(dst, p), "after", k1, k2)
                for p, k1, k2 in zip(back, leg1_ids, leg2_ids)
            ]
            self.help1, self.help2, self.help_z = [], [], help_z
            if help_z:
                marks = list(zip(back, leg1_ids, leg2_ids)) + list(zip(ahead, ahead_ids, ahead_ids))
                marks = marks[: len(help_z)]
                k, spot = fresh(), room[0]
                slot(max(p[1] for p, _, _ in marks))
                for j, (p, k1, k2) in enumerate(marks):
                    here = passing.at[pl.ds(spot, p[1])]
                    self.help1.append(remote(rows(src, p), here, at["helpers"][j], k1, k))
                    self.help2.append(remote(here, rows(dst, p), "help_end", k, k2))

        def send_ahead(self, i):
            if len(self.back) + i < len(self.help1):

                @pl.when(short)
                def _():
                    self.help1[len(self.back) + i].start()

                @pl.when(jnp.logical_not(short))
                def _():
                    self.straight[i].start()

            else:
                self.straight[i].start()

        def send_back(self, i):
            @pl.when(short)
            def _():
                (self.help1 if self.help1 else self.instead)[i].start()

            @pl.when(jnp.logical_not(short))
            def _():
                self.leg1[i].start()

        def relay(self, i):
            @pl.when(jnp.logical_not(idle))
            def _():
                self.leg1[i].wait_recv()
                self.leg2[i].start()

        def each_helper(self, act):
            for z_j, one, two in zip(self.help_z, self.help1, self.help2):

                @pl.when(helper & (at["z"] == z_j))
                def _():
                    act(one, two)

        def help(self):
            def act(one, two):
                one.wait_recv()
                two.start()

            self.each_helper(act)

        def wait_sends(self):
            for copy in self.straight + self.leg1:
                copy.wait_send()

            @pl.when(jnp.logical_not(idle))
            def _():
                for copy in self.leg2:
                    copy.wait_send()

            self.each_helper(lambda one, two: two.wait_send())

    texts = Stream(own, far_text, AHEAD_T, BACK_T, HELP_T.get(zs, ()))
    carries = Stream(carried, far_carried, AHEAD_C, BACK_C, HELP_C.get(zs, ()))
    ids_ahead = remote(ids, far_ids, "after")
    text_down = remote(own, mate_text, "mate")
    ids_down = remote(ids, mate_ids, "mate")
    arrivals = list(zip(texts.straight, AHEAD_T)) + list(zip(texts.leg2, BACK_T))
    text_up = [remote(rows(far_text, p), rows(mate_text, p), "mate") for _, p in arrivals]
    ids_up = remote(far_ids, mate_ids, "mate")
    part_over = remote(part, mate_part, "mate")

    def terms(text_block, text_ids, first, out):
        scale = jnp.exp(jnp.full((1, 256), log_scale[0], jnp.float32))
        shift = bias[0]
        image_ids = jnp.transpose(jnp.broadcast_to(ids[...].astype(jnp.float32), (128, 256)))
        other = text_ids[...].astype(jnp.float32)
        for i in range(2):
            at_rows = pl.ds(128 * i, 128)
            logits = (
                scale
                * lax.dot_general(
                    image[at_rows, :],
                    text_block[...],
                    (((1,), (1,)), ((), ())),
                    preferred_element_type=jnp.float32,
                )
                + shift
            )
            mine = image_ids[128 * i : 128 * (i + 1), 0:1]
            minus = jnp.where(mine == other, -1.0, 1.0)
            u = minus * logits
            e = jnp.exp(-jnp.abs(u))
            soft = jnp.maximum(u, 0.0) + jnp.log1p(e)
            sig = jnp.where(u >= 0, 1.0, e) / (1.0 + e)
            coef[at_rows, :] = (minus * sig * scale).astype(jnp.bfloat16)
            folded = soft[:, :128] + soft[:, 128:]
            if first:
                loss[at_rows, :] = folded
            else:
                loss[at_rows, :] = loss[at_rows, :] + folded
        for j in range(image.shape[1] // TILE):
            cols = pl.ds(TILE * j, TILE)
            g = jnp.dot(coef[...], text_block[:, cols], preferred_element_type=jnp.float32)
            if first:
                grad[:, cols] = g
            else:
                grad[:, cols] = grad[:, cols] + g
            out[:, cols] = lax.dot_general(
                coef[...],
                image[:, cols],
                (((0,), (0,)), ((), ())),
                preferred_element_type=jnp.float32,
            )

    loads[0].wait()
    own[...] = text[...].astype(jnp.bfloat16)
    for copy in loads[1:5]:
        copy.wait()
    terms(own, ids, True, total)
    loads[5].wait()

    @pl.when(is1)
    def _():
        carried[...] = (total[...] + accum[...]).astype(jnp.bfloat16)

    pl.semaphore_wait(barrier, partners)

    for i in range(max(len(BACK_T), len(AHEAD_T))):
        if i < len(BACK_T):
            texts.send_back(i)
        if i < len(AHEAD_T):
            texts.send_ahead(i)
        if i == 0:
            ids_ahead.start()

            @pl.when(is0)
            def _():
                text_down.start()
                ids_down.start()

    @pl.when(is1)
    def _():
        text_down.wait_recv()
        ids_down.wait_recv()
        terms(mate_text, mate_ids, False, part)
        part_over.start()

    @pl.when(is0)
    def _():
        part_over.wait_recv()
        carried[...] = (total[...] + accum[...] + mate_part[...]).astype(jnp.bfloat16)

    @pl.when(short)
    def _():
        for copy in carries.help1 or carries.instead:
            copy.start()

    for i in range(len(AHEAD_C)):
        carries.send_ahead(i)
    for i in range(max(len(BACK_T), len(BACK_C))):
        if i < len(BACK_T):
            texts.relay(i)
        if i < len(BACK_C):

            @pl.when(jnp.logical_not(short))
            def _():
                carries.leg1[i].start()
    texts.help()

    ids_ahead.wait_recv()

    @pl.when(is1)
    def _():
        ids_up.start()

    def relay_carries(first, end):
        for i in range(first, end):
            carries.relay(i)

    relay_carries(0, len(BACK_C))

    for i, (copy, _) in enumerate(arrivals):
        copy.wait_recv()

        @pl.when(is1)
        def _():
            text_up[i].start()

    carries.help()

    @pl.when(is0)
    def _():
        ids_up.wait_recv()
        for copy in text_up:
            copy.wait_recv()
        terms(mate_text, mate_ids, False, part)
        part_over.start()

    terms(far_text, far_ids, False, total)

    image_grad[...] = grad[...].astype(jnp.bfloat16)
    store_image = pltpu.make_async_copy(image_grad, image_grad_hbm, store_sem.at[0])
    store_image.start()
    columns = (SHIFTS + 1) * image.shape[0]
    loss_row[...] = jnp.sum(jnp.transpose(loss[...]), axis=0, keepdims=True) / columns
    store_loss = pltpu.make_async_copy(loss_row, loss_hbm, store_sem.at[1])
    store_loss.start()

    @pl.when(is1)
    def _():
        part_over.wait_recv()
        total[...] = total[...] + mate_part[...]

    stores = []

    def finish(copy, piece):
        copy.wait_recv()
        at_rows = pl.ds(piece[0], piece[1])
        total[at_rows, :] = total[at_rows, :] + far_carried[at_rows, :].astype(jnp.float32)
        store = pltpu.make_async_copy(
            rows(total, piece), rows(text_grad_hbm, piece), store_sem.at[2 + len(stores)]
        )
        store.start()
        stores.append(store)

    half = len(AHEAD_C) - len(BACK_C)
    for i in range(half):
        finish(carries.straight[i], AHEAD_C[i])
    for i in range(len(BACK_C)):
        finish(carries.leg2[i], BACK_C[i])
        finish(carries.straight[half + i], AHEAD_C[half + i])

    texts.wait_sends()
    carries.wait_sends()
    ids_ahead.wait_send()
    part_over.wait_send()

    @pl.when(is0)
    def _():
        text_down.wait_send()
        ids_down.wait_send()

    @pl.when(is1)
    def _():
        ids_up.wait_send()
        for copy in text_up:
            copy.wait_send()

    store_image.wait()
    store_loss.wait()
    for store in stores:
        store.wait()


def store_kernel(loss, image_grad, text_grad, loss_hbm, image_grad_hbm, text_grad_hbm, sem):
    copies = [
        pltpu.make_async_copy(src, dst, sem.at[i])
        for i, (src, dst) in enumerate(
            [(text_grad, text_grad_hbm), (image_grad, image_grad_hbm), (loss, loss_hbm)]
        )
    ]
    for copy in copies:
        copy.start()
    for copy in copies:
        copy.wait()


def solution(mesh):
    dps = mesh.shape["dp"]
    zs = max(dps // 8, 1)
    copies = 3 * len(BACK_T) + 2 * len(AHEAD_T) + len(AHEAD_C) + 2 * len(BACK_C) + 5
    copies += 2
    pieces = len(AHEAD_C) + len(BACK_C)
    passing_rows = sum(n for _, n in BACK_T) + sum(n for _, n in BACK_C)
    passing_rows += 32 + 16

    def body(image_emb, text_emb, text_accum, pair_ids, log_scale, bias):
        n, d = image_emb.shape
        any_space = pl.BlockSpec(memory_space=pl.ANY)
        hbm = pl.BlockSpec(memory_space=pltpu.HBM)
        f32, bf16, i32 = jnp.float32, jnp.bfloat16, jnp.int32
        shapes = (
            jax.ShapeDtypeStruct((1, n), f32),
            jax.ShapeDtypeStruct((n, d), bf16),
            jax.ShapeDtypeStruct((n, d), f32),
        )
        results = pl.pallas_call(
            functools.partial(kernel, zs, dps),
            out_shape=shapes,
            in_specs=[hbm] * 6,
            out_specs=(any_space, any_space, any_space),
            scratch_shapes=[
                pltpu.VMEM((n, d), bf16),
                pltpu.VMEM((n, d), f32),
                pltpu.VMEM((n, d), f32),
                pltpu.VMEM((n, d), bf16),
                pltpu.VMEM((n, d), bf16),
                pltpu.VMEM((n, d), bf16),
                pltpu.VMEM((n, n), bf16),
                pltpu.VMEM((n, d), f32),
                pltpu.VMEM((n, d), f32),
                pltpu.VMEM((n, d), f32),
                pltpu.VMEM((n, d), f32),
                pltpu.VMEM((n, d), bf16),
                pltpu.VMEM((n, d), bf16),
                pltpu.VMEM((passing_rows, d), bf16),
                pltpu.VMEM((n, 128), f32),
                pltpu.VMEM((1, n), f32),
                pltpu.VMEM((n, d), bf16),
                pltpu.VMEM((1, n), i32),
                pltpu.VMEM((1, n), i32),
                pltpu.VMEM((1, n), i32),
                pltpu.SMEM((1,), f32),
                pltpu.SMEM((1,), f32),
                pltpu.SemaphoreType.DMA((6,)),
                pltpu.SemaphoreType.DMA((2 + pieces,)),
                pltpu.SemaphoreType.DMA((copies,)),
                pltpu.SemaphoreType.DMA((copies,)),
            ],
            compiler_params=pltpu.CompilerParams(
                collective_id=0, has_side_effects=True, vmem_limit_bytes=51 << 20
            ),
        )(log_scale, bias, image_emb, text_emb, text_accum, pair_ids.reshape(1, n))
        loss, image_grad, text_grad = pl.pallas_call(
            store_kernel,
            out_shape=shapes,
            in_specs=[any_space] * 3,
            out_specs=(hbm, hbm, hbm),
            scratch_shapes=[pltpu.SemaphoreType.DMA((3,))],
            compiler_params=pltpu.CompilerParams(vmem_limit_bytes=1 << 20),
        )(*results)
        return loss.reshape(n), image_grad, text_grad

    split = P(("dp", "group"))
    wide = P(("dp", "group"), None)
    return jax.shard_map(
        body,
        mesh=mesh,
        in_specs=(wide, wide, wide, split, P(), P()),
        out_specs=(split, wide, wide),
        check_vma=False,
    )
```

```python
import functools

import jax
import jax.numpy as jnp
from jax import lax
from jax.experimental import pallas as pl
from jax.experimental.pallas import tpu as pltpu
from jax.sharding import PartitionSpec as P

SHIFTS = 2
Y = 8
TILE = 384
MESH = pl.DeviceIdType.MESH

AHEAD_T = [(64 + 32 * i, 32) for i in range(6)]
BACK_T = [(16 * i, 16) for i in range(4)]
AHEAD_C = [(48, 16)] + [(64 + 32 * i, 32) for i in range(5)] + [(224, 16), (240, 16)]
BACK_C = [(16 * i, 16) for i in range(3)]
HELP_T = {12: (1, 2, 3, 4, 5, 6, 7)}
HELP_C = {12: (1, 2, 3, 4, 5, 6, 7)}
HELP_T_6 = {12: (1, 2, 3, 4)}


def places(zs, dps):
    dp = lax.axis_index("dp")
    group = lax.axis_index("group")
    xs = max(dps // (2 * zs), 1)
    core = group % 2
    z = dp % zs
    y = (group // 2) * 2 + (dp // zs) % 2
    x = dp // (2 * zs)
    last = z == zs - 1
    helpers = (HELP_T_6.get(zs, ()), HELP_T.get(zs, ()))

    def chip(x, y, z):
        return ((x * 2 + y % 2) * zs + z, (y // 2) * 2 + core)

    def after(place):
        dp, group = place
        return ((dp + group // 6) % dps, (group + 2) % 8)

    def relay(x, y, z):
        turn = jnp.where((z == zs - 1) & (y == 6), 1, 0)
        return chip(x, (y + Y - 3 + turn) % Y, z)

    source = chip(x, (y + 3 - jnp.where(last & (y == 4), 1, 0)) % Y, z)
    previous = ((dp + dps - (7 - group) // 6) % dps, (group + 6) % 8)
    p_dp, p_group = previous
    p_z = p_dp % zs
    p_y = (p_group // 2) * 2 + (p_dp // zs) % 2
    helper = z < 0
    for low in (0, 1):
        for z_j in helpers[1 - low]:
            helper = helper | ((y == low) & (z == z_j))
    helped = chip(x, 7 - y, zs - 1)
    p_x = p_dp // (2 * zs)
    return dict(
        core=core,
        z=z,
        short=last & (y == 7),
        long=last & (y == 6),
        long_end=(p_z == zs - 1) & (p_y == 6),
        y=y,
        idle=last & (y == 3),
        end=(p_z == zs - 1) & (p_y == 7),
        late=(p_z == zs - 1) & (p_y >= 6),
        helper=helper,
        mate=(dp, group + 1 - 2 * core),
        after=after((dp, group)),
        previous=previous,
        via=relay(x, y, z),
        source=source,
        onward=after(source),
        previous_via=relay(p_dp // (2 * zs), p_y, p_z),
        helped=helped,
        help_end=after(helped),
        helpers=[[chip(x, 1 - k, z_j) for z_j in zz] for k, zz in enumerate(helpers)],
        end_helpers=[[chip(p_x, 1 - k, z_j) for z_j in zz] for k, zz in enumerate(helpers)],
    )


def kernel(
    zs,
    dps,
    log_scale_hbm,
    bias_hbm,
    image_hbm,
    text_hbm,
    accum_hbm,
    ids_hbm,
    loss_hbm,
    image_grad_hbm,
    text_grad_hbm,
    image,
    text,
    accum,
    own,
    mate_text,
    far_text,
    coef,
    grad,
    part,
    mate_part,
    total,
    carried,
    far_carried,
    passing,
    loss,
    loss_row,
    image_grad,
    ids,
    mate_ids,
    far_ids,
    log_scale,
    bias,
    load_sem,
    store_sem,
    sends,
    recvs,
):
    at = places(zs, dps)
    core = at["core"]
    is0 = core == 0
    is1 = core == 1
    short, idle, end, helper = at["short"], at["idle"], at["end"], at["helper"]
    helpers = (HELP_T_6.get(zs, ()), HELP_T.get(zs, ()))
    barrier = pltpu.get_barrier_semaphore()

    def greet(place):
        pl.semaphore_signal(barrier, inc=1, device_id=place, device_id_type=MESH)

    greet(at["mate"])
    greet(at["previous"])

    @pl.when(jnp.logical_not(idle))
    def _():
        greet(at["source"])

    @pl.when(jnp.logical_not(end))
    def _():
        greet(at["previous_via"])

    if helpers[1]:

        @pl.when(at["long_end"])
        def _():
            for place in at["end_helpers"][0]:
                greet(place)

        @pl.when(end)
        def _():
            for place in at["end_helpers"][1]:
                greet(place)

        @pl.when(helper)
        def _():
            greet(at["helped"])

    partners = 2 + jnp.where(short, len(helpers[1]), 1) + jnp.where(at["long"], len(helpers[0]), 0)
    partners += jnp.where(idle, 0, 1) + jnp.where(helper, 1, 0)

    loads = [
        pltpu.make_async_copy(src, dst, load_sem.at[i])
        for i, (src, dst) in enumerate(
            [
                (text_hbm, text),
                (image_hbm, image),
                (ids_hbm, ids),
                (log_scale_hbm, log_scale),
                (bias_hbm, bias),
                (accum_hbm, accum),
            ]
        )
    ]
    for copy in loads:
        copy.start()

    count = [0]

    def fresh():
        count[0] += 1
        return count[0] - 1

    def remote(src, dst, to, send=None, recv=None):
        k = fresh() if send is None or recv is None else 0
        return pltpu.make_async_remote_copy(
            src_ref=src,
            dst_ref=dst,
            send_sem=sends.at[k if send is None else send],
            recv_sem=recvs.at[k if recv is None else recv],
            device_id=at[to] if isinstance(to, str) else to,
            device_id_type=MESH,
        )

    def rows(ref, piece, shift=0):
        return ref.at[pl.ds(piece[0] + shift, piece[1])]

    room = [0]

    def slot(n):
        room[0] += n
        return passing.at[pl.ds(room[0] - n, n)]

    class Stream:
        def __init__(self, src, dst, ahead, back, help_z, help_z_6=()):
            self.ahead, self.back = ahead, back
            ahead_ids = [fresh() for _ in ahead]
            leg1_ids = [fresh() for _ in back]
            leg2_ids = [fresh() for _ in back]
            self.straight = [
                remote(rows(src, p), rows(dst, p), "after", k, k) for p, k in zip(ahead, ahead_ids)
            ]
            slots = [slot(n) for _, n in back]
            self.leg1 = [
                remote(rows(src, p), t, "via", k, k) for p, t, k in zip(back, slots, leg1_ids)
            ]
            self.leg2 = [
                remote(t, rows(dst, p), "onward", k, k) for p, t, k in zip(back, slots, leg2_ids)
            ]
            self.instead = [
                remote(rows(src, p), rows(dst, p), "after", k1, k2)
                for p, k1, k2 in zip(back, leg1_ids, leg2_ids)
            ]
            self.help1, self.help2, self.help_z = [], [], help_z
            self.six1, self.six2, self.help_z_6 = {}, {}, help_z_6
            if help_z:
                marks = list(zip(back, leg1_ids, leg2_ids)) + list(zip(ahead, ahead_ids, ahead_ids))
                marks = marks[: len(help_z)]
                k, spot = fresh(), room[0]
                slot(max(p[1] for p, _, _ in marks))

                def pair(p, k1, k2, place):
                    here = passing.at[pl.ds(spot, p[1])]
                    return (
                        remote(rows(src, p), here, place, k1, k),
                        remote(here, rows(dst, p), "help_end", k, k2),
                    )

                for j, (p, k1, k2) in enumerate(marks):
                    one, two = pair(p, k1, k2, at["helpers"][1][j])
                    self.help1.append(one)
                    self.help2.append(two)
                for j in range(len(help_z_6)):
                    i = len(ahead) - 1 - j
                    place = at["helpers"][0][j]
                    self.six1[i], self.six2[i] = pair(ahead[i], ahead_ids[i], ahead_ids[i], place)

        def send_ahead(self, i, helped=True):
            straight = None
            j = len(self.back) + i
            if j < len(self.help1):
                straight = jnp.logical_not(short)
                if helped:

                    @pl.when(short)
                    def _():
                        self.help1[j].start()

            if i in self.six1:
                long = at["long"]
                other = jnp.logical_not(long)
                straight = other if straight is None else straight & other

                @pl.when(long)
                def _():
                    self.six1[i].start()

            if straight is None:
                self.straight[i].start()
            else:

                @pl.when(straight)
                def _():
                    self.straight[i].start()

        def send_back(self, i):
            @pl.when(short)
            def _():
                (self.help1 if self.help1 else self.instead)[i].start()

            @pl.when(jnp.logical_not(short))
            def _():
                self.leg1[i].start()

        def relay(self, i):
            @pl.when(jnp.logical_not(idle))
            def _():
                self.leg1[i].wait_recv()
                self.leg2[i].start()

        def each_helper(self, act):
            for z_j, one, two in zip(self.help_z, self.help1, self.help2):

                @pl.when((at["y"] == 0) & (at["z"] == z_j))
                def _():
                    act(one, two)

            for z_j, one, two in zip(self.help_z_6, self.six1.values(), self.six2.values()):

                @pl.when((at["y"] == 1) & (at["z"] == z_j))
                def _():
                    act(one, two)

        def help(self):
            def act(one, two):
                one.wait_recv()
                two.start()

            self.each_helper(act)

        def wait_sends(self):
            for copy in self.straight + self.leg1:
                copy.wait_send()

            @pl.when(jnp.logical_not(idle))
            def _():
                for copy in self.leg2:
                    copy.wait_send()

            self.each_helper(lambda one, two: two.wait_send())

    texts = Stream(
        own, far_text, AHEAD_T, BACK_T, HELP_T.get(zs, ()), HELP_T_6.get(zs, ())
    )
    carries = Stream(carried, far_carried, AHEAD_C, BACK_C, HELP_C.get(zs, ()))
    ids_ahead = remote(ids, far_ids, "after")
    text_down = remote(own, mate_text, "mate")
    ids_down = remote(ids, mate_ids, "mate")
    arrivals = list(zip(texts.straight, AHEAD_T)) + list(zip(texts.leg2, BACK_T))
    text_up = [remote(rows(far_text, p), rows(mate_text, p), "mate") for _, p in arrivals]
    ids_up = remote(far_ids, mate_ids, "mate")
    part_over = remote(part, mate_part, "mate")

    def terms(text_block, text_ids, first, out):
        scale = jnp.exp(jnp.full((1, 256), log_scale[0], jnp.float32))
        shift = bias[0]
        image_ids = jnp.transpose(jnp.broadcast_to(ids[...].astype(jnp.float32), (128, 256)))
        other = text_ids[...].astype(jnp.float32)
        for i in range(2):
            at_rows = pl.ds(128 * i, 128)
            logits = (
                scale
                * lax.dot_general(
                    image[at_rows, :],
                    text_block[...],
                    (((1,), (1,)), ((), ())),
                    preferred_element_type=jnp.float32,
                )
                + shift
            )
            mine = image_ids[128 * i : 128 * (i + 1), 0:1]
            minus = jnp.where(mine == other, -1.0, 1.0)
            u = minus * logits
            e = jnp.exp(-jnp.abs(u))
            soft = jnp.maximum(u, 0.0) + jnp.log1p(e)
            sig = jnp.where(u >= 0, 1.0, e) / (1.0 + e)
            coef[at_rows, :] = (minus * sig * scale).astype(jnp.bfloat16)
            folded = soft[:, :128] + soft[:, 128:]
            if first:
                loss[at_rows, :] = folded
            else:
                loss[at_rows, :] = loss[at_rows, :] + folded
        for j in range(image.shape[1] // TILE):
            cols = pl.ds(TILE * j, TILE)
            g = jnp.dot(coef[...], text_block[:, cols], preferred_element_type=jnp.float32)
            if first:
                grad[:, cols] = g
            else:
                grad[:, cols] = grad[:, cols] + g
            out[:, cols] = lax.dot_general(
                coef[...],
                image[:, cols],
                (((0,), (0,)), ((), ())),
                preferred_element_type=jnp.float32,
            )

    loads[0].wait()
    own[...] = text[...].astype(jnp.bfloat16)
    for copy in loads[1:5]:
        copy.wait()
    terms(own, ids, True, total)
    loads[5].wait()

    @pl.when(is1)
    def _():
        carried[...] = (total[...] + accum[...]).astype(jnp.bfloat16)

    pl.semaphore_wait(barrier, partners)

    for i in range(max(len(BACK_T), len(AHEAD_T))):
        if i < len(BACK_T):
            texts.send_back(i)
        if i < len(AHEAD_T):
            texts.send_ahead(i)
        if i == 0:
            ids_ahead.start()

            @pl.when(is0)
            def _():
                text_down.start()
                ids_down.start()

    @pl.when(is1)
    def _():
        text_down.wait_recv()
        ids_down.wait_recv()
        terms(mate_text, mate_ids, False, part)
        part_over.start()

    @pl.when(is0)
    def _():
        part_over.wait_recv()
        carried[...] = (total[...] + accum[...] + mate_part[...]).astype(jnp.bfloat16)

    @pl.when(short)
    def _():
        for copy in carries.help1 or carries.instead:
            copy.start()

    for i in range(len(AHEAD_C)):
        carries.send_ahead(i, helped=False)
    for i in range(max(len(BACK_T), len(BACK_C))):
        if i < len(BACK_T):
            texts.relay(i)
        if i < len(BACK_C):

            @pl.when(jnp.logical_not(short))
            def _():
                carries.leg1[i].start()
    texts.help()

    ids_ahead.wait_recv()

    @pl.when(is1)
    def _():
        ids_up.start()

    def relay_carries(first, end):
        for i in range(first, end):
            carries.relay(i)

    half = len(BACK_C) // 2
    relay_carries(0, half)
    carries.help()
    relay_carries(half, len(BACK_C))

    for i, (copy, _) in enumerate(arrivals):
        copy.wait_recv()

        @pl.when(is1)
        def _():
            text_up[i].start()

    @pl.when(is0)
    def _():
        ids_up.wait_recv()
        for copy in text_up:
            copy.wait_recv()
        terms(mate_text, mate_ids, False, part)
        part_over.start()

    terms(far_text, far_ids, False, total)

    image_grad[...] = grad[...].astype(jnp.bfloat16)
    store_image = pltpu.make_async_copy(image_grad, image_grad_hbm, store_sem.at[0])
    store_image.start()
    columns = (SHIFTS + 1) * image.shape[0]
    loss_row[...] = jnp.sum(jnp.transpose(loss[...]), axis=0, keepdims=True) / columns
    store_loss = pltpu.make_async_copy(loss_row, loss_hbm, store_sem.at[1])
    store_loss.start()

    @pl.when(is1)
    def _():
        part_over.wait_recv()
        total[...] = total[...] + mate_part[...]

    stores = []

    def finish(copy, piece):
        copy.wait_recv()
        at_rows = pl.ds(piece[0], piece[1])
        total[at_rows, :] = total[at_rows, :] + far_carried[at_rows, :].astype(jnp.float32)
        store = pltpu.make_async_copy(
            rows(total, piece), rows(text_grad_hbm, piece), store_sem.at[2 + len(stores)]
        )
        store.start()
        stores.append(store)

    half = len(AHEAD_C) - len(BACK_C)
    for i in range(half):
        finish(carries.straight[i], AHEAD_C[i])
    for i in range(len(BACK_C)):
        finish(carries.leg2[i], BACK_C[i])
        finish(carries.straight[half + i], AHEAD_C[half + i])

    texts.wait_sends()
    carries.wait_sends()
    ids_ahead.wait_send()
    part_over.wait_send()

    @pl.when(is0)
    def _():
        text_down.wait_send()
        ids_down.wait_send()

    @pl.when(is1)
    def _():
        ids_up.wait_send()
        for copy in text_up:
            copy.wait_send()

    store_image.wait()
    store_loss.wait()
    for store in stores:
        store.wait()


def store_kernel(loss, image_grad, text_grad, loss_hbm, image_grad_hbm, text_grad_hbm, sem):
    copies = [
        pltpu.make_async_copy(src, dst, sem.at[i])
        for i, (src, dst) in enumerate(
            [(text_grad, text_grad_hbm), (image_grad, image_grad_hbm), (loss, loss_hbm)]
        )
    ]
    for copy in copies:
        copy.start()
    for copy in copies:
        copy.wait()


def solution(mesh):
    dps = mesh.shape["dp"]
    zs = max(dps // 8, 1)
    copies = 3 * len(BACK_T) + 2 * len(AHEAD_T) + len(AHEAD_C) + 2 * len(BACK_C) + 5
    copies += 2
    pieces = len(AHEAD_C) + len(BACK_C)
    passing_rows = sum(n for _, n in BACK_T) + sum(n for _, n in BACK_C)
    passing_rows += 32 + 32

    def body(image_emb, text_emb, text_accum, pair_ids, log_scale, bias):
        n, d = image_emb.shape
        any_space = pl.BlockSpec(memory_space=pl.ANY)
        hbm = pl.BlockSpec(memory_space=pltpu.HBM)
        f32, bf16, i32 = jnp.float32, jnp.bfloat16, jnp.int32
        shapes = (
            jax.ShapeDtypeStruct((1, n), f32),
            jax.ShapeDtypeStruct((n, d), bf16),
            jax.ShapeDtypeStruct((n, d), f32),
        )
        results = pl.pallas_call(
            functools.partial(kernel, zs, dps),
            out_shape=shapes,
            in_specs=[hbm] * 6,
            out_specs=(any_space, any_space, any_space),
            scratch_shapes=[
                pltpu.VMEM((n, d), bf16),
                pltpu.VMEM((n, d), f32),
                pltpu.VMEM((n, d), f32),
                pltpu.VMEM((n, d), bf16),
                pltpu.VMEM((n, d), bf16),
                pltpu.VMEM((n, d), bf16),
                pltpu.VMEM((n, n), bf16),
                pltpu.VMEM((n, d), f32),
                pltpu.VMEM((n, d), f32),
                pltpu.VMEM((n, d), f32),
                pltpu.VMEM((n, d), f32),
                pltpu.VMEM((n, d), bf16),
                pltpu.VMEM((n, d), bf16),
                pltpu.VMEM((passing_rows, d), bf16),
                pltpu.VMEM((n, 128), f32),
                pltpu.VMEM((1, n), f32),
                pltpu.VMEM((n, d), bf16),
                pltpu.VMEM((1, n), i32),
                pltpu.VMEM((1, n), i32),
                pltpu.VMEM((1, n), i32),
                pltpu.SMEM((1,), f32),
                pltpu.SMEM((1,), f32),
                pltpu.SemaphoreType.DMA((6,)),
                pltpu.SemaphoreType.DMA((2 + pieces,)),
                pltpu.SemaphoreType.DMA((copies,)),
                pltpu.SemaphoreType.DMA((copies,)),
            ],
            compiler_params=pltpu.CompilerParams(
                collective_id=0, has_side_effects=True, vmem_limit_bytes=51 << 20
            ),
        )(log_scale, bias, image_emb, text_emb, text_accum, pair_ids.reshape(1, n))
        loss, image_grad, text_grad = pl.pallas_call(
            store_kernel,
            out_shape=shapes,
            in_specs=[any_space] * 3,
            out_specs=(hbm, hbm, hbm),
            scratch_shapes=[pltpu.SemaphoreType.DMA((3,))],
            compiler_params=pltpu.CompilerParams(vmem_limit_bytes=1 << 20),
        )(*results)
        return loss.reshape(n), image_grad, text_grad

    split = P(("dp", "group"))
    wide = P(("dp", "group"), None)
    return jax.shard_map(
        body,
        mesh=mesh,
        in_specs=(wide, wide, wide, split, P(), P()),
        out_specs=(split, wide, wide),
        check_vma=False,
    )
```

```python
import functools

import jax
import jax.numpy as jnp
from jax import lax
from jax.experimental import pallas as pl
from jax.experimental.pallas import tpu as pltpu
from jax.sharding import PartitionSpec as P

SHIFTS = 2
Y = 8
TILE = 384
MESH = pl.DeviceIdType.MESH

AHEAD_T = [(64 + 32 * i, 32) for i in range(6)]
BACK_T = [(16 * i, 16) for i in range(4)]
AHEAD_C = [(48, 16)] + [(64 + 32 * i, 32) for i in range(5)] + [(224, 16), (240, 16)]
BACK_C = [(16 * i, 16) for i in range(3)]
HELP_T = {12: (1, 2, 3, 4, 5, 6, 7)}
HELP_C = {12: (1, 2, 3, 4, 5, 6, 7)}
HELP_T_6 = {12: (1, 2, 3, 4)}


def places(zs, dps):
    dp = lax.axis_index("dp")
    group = lax.axis_index("group")
    xs = max(dps // (2 * zs), 1)
    core = group % 2
    z = dp % zs
    y = (group // 2) * 2 + (dp // zs) % 2
    x = dp // (2 * zs)
    last = z == zs - 1
    helpers = (HELP_T_6.get(zs, ()), HELP_T.get(zs, ()))

    def chip(x, y, z):
        return ((x * 2 + y % 2) * zs + z, (y // 2) * 2 + core)

    def after(place):
        dp, group = place
        return ((dp + group // 6) % dps, (group + 2) % 8)

    def relay(x, y, z):
        turn = jnp.where((z == zs - 1) & (y == 6), 1, 0)
        return chip(x, (y + Y - 3 + turn) % Y, z)

    source = chip(x, (y + 3 - jnp.where(last & (y == 4), 1, 0)) % Y, z)
    previous = ((dp + dps - (7 - group) // 6) % dps, (group + 6) % 8)
    p_dp, p_group = previous
    p_z = p_dp % zs
    p_y = (p_group // 2) * 2 + (p_dp // zs) % 2
    helper = z < 0
    for low in (0, 1):
        for z_j in helpers[1 - low]:
            helper = helper | ((y == low) & (z == z_j))
    helped = chip(x, 7 - y, zs - 1)
    p_x = p_dp // (2 * zs)
    return dict(
        core=core,
        z=z,
        short=last & (y == 7),
        long=last & (y == 6),
        long_end=(p_z == zs - 1) & (p_y == 6),
        y=y,
        idle=last & (y == 3),
        end=(p_z == zs - 1) & (p_y == 7),
        late=(p_z == zs - 1) & (p_y >= 6),
        helper=helper,
        mate=(dp, group + 1 - 2 * core),
        after=after((dp, group)),
        previous=previous,
        via=relay(x, y, z),
        source=source,
        onward=after(source),
        previous_via=relay(p_dp // (2 * zs), p_y, p_z),
        helped=helped,
        help_end=after(helped),
        helpers=[[chip(x, 1 - k, z_j) for z_j in zz] for k, zz in enumerate(helpers)],
        end_helpers=[[chip(p_x, 1 - k, z_j) for z_j in zz] for k, zz in enumerate(helpers)],
    )


def kernel(
    zs,
    dps,
    log_scale_hbm,
    bias_hbm,
    image_hbm,
    text_hbm,
    accum_hbm,
    ids_hbm,
    loss_hbm,
    image_grad_hbm,
    text_grad_top,
    text_grad_bottom,
    image,
    text,
    accum,
    own,
    mate_text,
    far_text,
    coef,
    grad,
    part,
    mate_part,
    total,
    carried,
    far_carried,
    passing,
    loss,
    loss_row,
    image_grad,
    ids,
    mate_ids,
    far_ids,
    log_scale,
    bias,
    load_sem,
    store_sem,
    sends,
    recvs,
):
    at = places(zs, dps)
    core = at["core"]
    is0 = core == 0
    is1 = core == 1
    short, idle, end, helper = at["short"], at["idle"], at["end"], at["helper"]
    helpers = (HELP_T_6.get(zs, ()), HELP_T.get(zs, ()))
    barrier = pltpu.get_barrier_semaphore()

    def greet(place):
        pl.semaphore_signal(barrier, inc=1, device_id=place, device_id_type=MESH)

    greet(at["mate"])
    greet(at["previous"])

    @pl.when(jnp.logical_not(idle))
    def _():
        greet(at["source"])

    @pl.when(jnp.logical_not(end))
    def _():
        greet(at["previous_via"])

    if helpers[1]:

        @pl.when(at["long_end"])
        def _():
            for place in at["end_helpers"][0]:
                greet(place)

        @pl.when(end)
        def _():
            for place in at["end_helpers"][1]:
                greet(place)

        @pl.when(helper)
        def _():
            greet(at["helped"])

    partners = 2 + jnp.where(short, len(helpers[1]), 1) + jnp.where(at["long"], len(helpers[0]), 0)
    partners += jnp.where(idle, 0, 1) + jnp.where(helper, 1, 0)

    loads = [
        pltpu.make_async_copy(src, dst, load_sem.at[i])
        for i, (src, dst) in enumerate(
            [
                (text_hbm, text),
                (image_hbm, image),
                (ids_hbm, ids),
                (log_scale_hbm, log_scale),
                (bias_hbm, bias),
                (accum_hbm, accum),
            ]
        )
    ]
    for copy in loads:
        copy.start()

    count = [0]

    def fresh():
        count[0] += 1
        return count[0] - 1

    def remote(src, dst, to, send=None, recv=None):
        k = fresh() if send is None or recv is None else 0
        return pltpu.make_async_remote_copy(
            src_ref=src,
            dst_ref=dst,
            send_sem=sends.at[k if send is None else send],
            recv_sem=recvs.at[k if recv is None else recv],
            device_id=at[to] if isinstance(to, str) else to,
            device_id_type=MESH,
        )

    def rows(ref, piece, shift=0):
        return ref.at[pl.ds(piece[0] + shift, piece[1])]

    room = [0]

    def slot(n):
        room[0] += n
        return passing.at[pl.ds(room[0] - n, n)]

    class Stream:
        def __init__(self, src, dst, ahead, back, help_z, help_z_6=()):
            self.ahead, self.back = ahead, back
            ahead_ids = [fresh() for _ in ahead]
            leg1_ids = [fresh() for _ in back]
            leg2_ids = [fresh() for _ in back]
            self.straight = [
                remote(rows(src, p), rows(dst, p), "after", k, k) for p, k in zip(ahead, ahead_ids)
            ]
            slots = [slot(n) for _, n in back]
            self.leg1 = [
                remote(rows(src, p), t, "via", k, k) for p, t, k in zip(back, slots, leg1_ids)
            ]
            self.leg2 = [
                remote(t, rows(dst, p), "onward", k, k) for p, t, k in zip(back, slots, leg2_ids)
            ]
            self.instead = [
                remote(rows(src, p), rows(dst, p), "after", k1, k2)
                for p, k1, k2 in zip(back, leg1_ids, leg2_ids)
            ]
            self.help1, self.help2, self.help_z = [], [], help_z
            self.six1, self.six2, self.help_z_6 = {}, {}, help_z_6
            if help_z:
                marks = list(zip(back, leg1_ids, leg2_ids)) + list(zip(ahead, ahead_ids, ahead_ids))
                marks = marks[: len(help_z)]
                k, spot = fresh(), room[0]
                slot(max(p[1] for p, _, _ in marks))

                def pair(p, k1, k2, place):
                    here = passing.at[pl.ds(spot, p[1])]
                    return (
                        remote(rows(src, p), here, place, k1, k),
                        remote(here, rows(dst, p), "help_end", k, k2),
                    )

                for j, (p, k1, k2) in enumerate(marks):
                    one, two = pair(p, k1, k2, at["helpers"][1][j])
                    self.help1.append(one)
                    self.help2.append(two)
                for j in range(len(help_z_6)):
                    i = len(ahead) - 1 - j
                    place = at["helpers"][0][j]
                    self.six1[i], self.six2[i] = pair(ahead[i], ahead_ids[i], ahead_ids[i], place)

        def send_ahead(self, i, helped=True):
            straight = None
            j = len(self.back) + i
            if j < len(self.help1):
                straight = jnp.logical_not(short)
                if helped:

                    @pl.when(short)
                    def _():
                        self.help1[j].start()

            if i in self.six1:
                long = at["long"]
                other = jnp.logical_not(long)
                straight = other if straight is None else straight & other

                @pl.when(long)
                def _():
                    self.six1[i].start()

            if straight is None:
                self.straight[i].start()
            else:

                @pl.when(straight)
                def _():
                    self.straight[i].start()

        def send_back(self, i):
            @pl.when(short)
            def _():
                (self.help1 if self.help1 else self.instead)[i].start()

            @pl.when(jnp.logical_not(short))
            def _():
                self.leg1[i].start()

        def relay(self, i):
            @pl.when(jnp.logical_not(idle))
            def _():
                self.leg1[i].wait_recv()
                self.leg2[i].start()

        def each_helper(self, act):
            for z_j, one, two in zip(self.help_z, self.help1, self.help2):

                @pl.when((at["y"] == 0) & (at["z"] == z_j))
                def _():
                    act(one, two)

            for z_j, one, two in zip(self.help_z_6, self.six1.values(), self.six2.values()):

                @pl.when((at["y"] == 1) & (at["z"] == z_j))
                def _():
                    act(one, two)

        def help(self):
            def act(one, two):
                one.wait_recv()
                two.start()

            self.each_helper(act)

        def wait_sends(self):
            for copy in self.straight + self.leg1:
                copy.wait_send()

            @pl.when(jnp.logical_not(idle))
            def _():
                for copy in self.leg2:
                    copy.wait_send()

            self.each_helper(lambda one, two: two.wait_send())

    texts = Stream(
        own, far_text, AHEAD_T, BACK_T, HELP_T.get(zs, ()), HELP_T_6.get(zs, ())
    )
    carries = Stream(carried, far_carried, AHEAD_C, BACK_C, HELP_C.get(zs, ()))
    ids_ahead = remote(ids, far_ids, "after")
    text_down = remote(own, mate_text, "mate")
    ids_down = remote(ids, mate_ids, "mate")
    arrivals = list(zip(texts.straight, AHEAD_T)) + list(zip(texts.leg2, BACK_T))
    text_up = [remote(rows(far_text, p), rows(mate_text, p), "mate") for _, p in arrivals]
    ids_up = remote(far_ids, mate_ids, "mate")
    part_over = remote(part, mate_part, "mate")

    def terms(text_block, text_ids, first, out):
        scale = jnp.exp(jnp.full((1, 256), log_scale[0], jnp.float32))
        shift = bias[0]
        image_ids = jnp.transpose(jnp.broadcast_to(ids[...].astype(jnp.float32), (128, 256)))
        other = text_ids[...].astype(jnp.float32)
        for i in range(2):
            at_rows = pl.ds(128 * i, 128)
            logits = (
                scale
                * lax.dot_general(
                    image[at_rows, :],
                    text_block[...],
                    (((1,), (1,)), ((), ())),
                    preferred_element_type=jnp.float32,
                )
                + shift
            )
            mine = image_ids[128 * i : 128 * (i + 1), 0:1]
            minus = jnp.where(mine == other, -1.0, 1.0)
            u = minus * logits
            e = jnp.exp(-jnp.abs(u))
            soft = jnp.maximum(u, 0.0) + jnp.log1p(e)
            sig = jnp.where(u >= 0, 1.0, e) / (1.0 + e)
            coef[at_rows, :] = (minus * sig * scale).astype(jnp.bfloat16)
            folded = soft[:, :128] + soft[:, 128:]
            if first:
                loss[at_rows, :] = folded
            else:
                loss[at_rows, :] = loss[at_rows, :] + folded
        for j in range(image.shape[1] // TILE):
            cols = pl.ds(TILE * j, TILE)
            g = jnp.dot(coef[...], text_block[:, cols], preferred_element_type=jnp.float32)
            if first:
                grad[:, cols] = g
            else:
                grad[:, cols] = grad[:, cols] + g
            out[:, cols] = lax.dot_general(
                coef[...],
                image[:, cols],
                (((0,), (0,)), ((), ())),
                preferred_element_type=jnp.float32,
            )

    loads[0].wait()
    own[...] = text[...].astype(jnp.bfloat16)
    for copy in loads[1:5]:
        copy.wait()
    terms(own, ids, True, total)
    loads[5].wait()

    @pl.when(is1)
    def _():
        carried[...] = (total[...] + accum[...]).astype(jnp.bfloat16)

    pl.semaphore_wait(barrier, partners)

    for i in range(max(len(BACK_T), len(AHEAD_T))):
        if i < len(BACK_T):
            texts.send_back(i)
        if i < len(AHEAD_T):
            texts.send_ahead(i)
        if i == 0:
            ids_ahead.start()

            @pl.when(is0)
            def _():
                text_down.start()
                ids_down.start()

    @pl.when(is1)
    def _():
        text_down.wait_recv()
        ids_down.wait_recv()
        terms(mate_text, mate_ids, False, part)
        part_over.start()

    @pl.when(is0)
    def _():
        part_over.wait_recv()
        carried[...] = (total[...] + accum[...] + mate_part[...]).astype(jnp.bfloat16)

    @pl.when(short)
    def _():
        for copy in carries.help1 or carries.instead:
            copy.start()

    for i in range(len(AHEAD_C)):
        carries.send_ahead(i, helped=False)
    for i in range(max(len(BACK_T), len(BACK_C))):
        if i < len(BACK_T):
            texts.relay(i)
        if i < len(BACK_C):

            @pl.when(jnp.logical_not(short))
            def _():
                carries.leg1[i].start()
    texts.help()

    ids_ahead.wait_recv()

    @pl.when(is1)
    def _():
        ids_up.start()

    def relay_carries(first, end):
        for i in range(first, end):
            carries.relay(i)

    half = len(BACK_C) // 2
    relay_carries(0, half)
    carries.help()
    relay_carries(half, len(BACK_C))

    for i, (copy, _) in enumerate(arrivals):
        copy.wait_recv()

        @pl.when(is1)
        def _():
            text_up[i].start()

    @pl.when(is0)
    def _():
        ids_up.wait_recv()
        for copy in text_up:
            copy.wait_recv()
        terms(mate_text, mate_ids, False, part)
        part_over.start()

    terms(far_text, far_ids, False, total)

    image_grad[...] = grad[...].astype(jnp.bfloat16)
    store_image = pltpu.make_async_copy(image_grad, image_grad_hbm, store_sem.at[0])
    store_image.start()
    columns = (SHIFTS + 1) * image.shape[0]
    loss_row[...] = jnp.sum(jnp.transpose(loss[...]), axis=0, keepdims=True) / columns
    store_loss = pltpu.make_async_copy(loss_row, loss_hbm, store_sem.at[1])
    store_loss.start()

    @pl.when(is1)
    def _():
        part_over.wait_recv()
        total[...] = total[...] + mate_part[...]

    stores = []

    def finish(copy, piece):
        copy.wait_recv()
        at_rows = pl.ds(piece[0], piece[1])
        total[at_rows, :] = total[at_rows, :] + far_carried[at_rows, :].astype(jnp.float32)
        middle = total.shape[0] // 2
        top = piece[0] < middle
        place = rows(text_grad_top, piece) if top else rows(text_grad_bottom, piece, -middle)
        store = pltpu.make_async_copy(rows(total, piece), place, store_sem.at[2 + len(stores)])
        store.start()
        stores.append(store)

    half = len(AHEAD_C) - len(BACK_C)
    for i in range(half):
        finish(carries.straight[i], AHEAD_C[i])
    for i in range(len(BACK_C)):
        finish(carries.leg2[i], BACK_C[i])
        finish(carries.straight[half + i], AHEAD_C[half + i])

    texts.wait_sends()
    carries.wait_sends()
    ids_ahead.wait_send()
    part_over.wait_send()

    @pl.when(is0)
    def _():
        text_down.wait_send()
        ids_down.wait_send()

    @pl.when(is1)
    def _():
        ids_up.wait_send()
        for copy in text_up:
            copy.wait_send()

    store_image.wait()
    store_loss.wait()
    for store in stores:
        store.wait()


def store_kernel(loss, image_grad, top, bottom, loss_hbm, image_grad_hbm, text_grad_hbm, sem):
    middle = top.shape[0]
    pairs = [
        (top, text_grad_hbm.at[pl.ds(0, middle)]),
        (bottom, text_grad_hbm.at[pl.ds(middle, middle)]),
        (image_grad, image_grad_hbm),
        (loss, loss_hbm),
    ]
    copies = [pltpu.make_async_copy(src, dst, sem.at[i]) for i, (src, dst) in enumerate(pairs)]
    for copy in copies:
        copy.start()
    for copy in copies:
        copy.wait()


def solution(mesh):
    dps = mesh.shape["dp"]
    zs = max(dps // 8, 1)
    copies = 3 * len(BACK_T) + 2 * len(AHEAD_T) + len(AHEAD_C) + 2 * len(BACK_C) + 5
    copies += 2
    pieces = len(AHEAD_C) + len(BACK_C)
    passing_rows = sum(n for _, n in BACK_T) + sum(n for _, n in BACK_C)
    passing_rows += 32 + 32

    def body(image_emb, text_emb, text_accum, pair_ids, log_scale, bias):
        n, d = image_emb.shape
        any_space = pl.BlockSpec(memory_space=pl.ANY)
        hbm = pl.BlockSpec(memory_space=pltpu.HBM)
        f32, bf16, i32 = jnp.float32, jnp.bfloat16, jnp.int32
        shapes = (
            jax.ShapeDtypeStruct((1, n), f32),
            jax.ShapeDtypeStruct((n, d), bf16),
            jax.ShapeDtypeStruct((n, d), f32),
        )
        results = pl.pallas_call(
            functools.partial(kernel, zs, dps),
            out_shape=shapes[:2] + (jax.ShapeDtypeStruct((n // 2, d), f32),) * 2,
            in_specs=[hbm] * 6,
            out_specs=(any_space,) * 4,
            scratch_shapes=[
                pltpu.VMEM((n, d), bf16),
                pltpu.VMEM((n, d), f32),
                pltpu.VMEM((n, d), f32),
                pltpu.VMEM((n, d), bf16),
                pltpu.VMEM((n, d), bf16),
                pltpu.VMEM((n, d), bf16),
                pltpu.VMEM((n, n), bf16),
                pltpu.VMEM((n, d), f32),
                pltpu.VMEM((n, d), f32),
                pltpu.VMEM((n, d), f32),
                pltpu.VMEM((n, d), f32),
                pltpu.VMEM((n, d), bf16),
                pltpu.VMEM((n, d), bf16),
                pltpu.VMEM((passing_rows, d), bf16),
                pltpu.VMEM((n, 128), f32),
                pltpu.VMEM((1, n), f32),
                pltpu.VMEM((n, d), bf16),
                pltpu.VMEM((1, n), i32),
                pltpu.VMEM((1, n), i32),
                pltpu.VMEM((1, n), i32),
                pltpu.SMEM((1,), f32),
                pltpu.SMEM((1,), f32),
                pltpu.SemaphoreType.DMA((6,)),
                pltpu.SemaphoreType.DMA((2 + pieces,)),
                pltpu.SemaphoreType.DMA((copies,)),
                pltpu.SemaphoreType.DMA((copies,)),
            ],
            compiler_params=pltpu.CompilerParams(
                collective_id=0, has_side_effects=True, vmem_limit_bytes=53120 << 10
            ),
        )(log_scale, bias, image_emb, text_emb, text_accum, pair_ids.reshape(1, n))
        loss, image_grad, text_grad = pl.pallas_call(
            store_kernel,
            out_shape=shapes,
            in_specs=[any_space] * 4,
            out_specs=(hbm, hbm, hbm),
            scratch_shapes=[pltpu.SemaphoreType.DMA((4,))],
            compiler_params=pltpu.CompilerParams(vmem_limit_bytes=1 << 20),
        )(*results)
        return loss.reshape(n), image_grad, text_grad

    split = P(("dp", "group"))
    wide = P(("dp", "group"), None)
    return jax.shard_map(
        body,
        mesh=mesh,
        in_specs=(wide, wide, wide, split, P(), P()),
        out_specs=(split, wide, wide),
        check_vma=False,
    )
```

```python
import functools

import jax
import jax.numpy as jnp
from jax import lax
from jax.experimental import pallas as pl
from jax.experimental.pallas import tpu as pltpu
from jax.sharding import PartitionSpec as P

SHIFTS = 2
Y = 8
TILE = 384
MESH = pl.DeviceIdType.MESH

AHEAD_T = [(64 + 32 * i, 32) for i in range(6)]
BACK_T = [(16 * i, 16) for i in range(4)]
AHEAD_C = [(48, 16)] + [(64 + 32 * i, 32) for i in range(5)] + [(224, 16), (240, 16)]
BACK_C = [(16 * i, 16) for i in range(3)]
HELP_T = {12: (1, 2, 3, 4, 5, 6, 7)}
HELP_C = {12: (1, 2, 3, 4, 5, 6, 7)}
HELP_T_6 = {12: (1, 2, 3, 4)}
HELP_C_6 = {12: (1, 2, 3)}


def places(zs, dps):
    dp = lax.axis_index("dp")
    group = lax.axis_index("group")
    xs = max(dps // (2 * zs), 1)
    core = group % 2
    z = dp % zs
    y = (group // 2) * 2 + (dp // zs) % 2
    x = dp // (2 * zs)
    last = z == zs - 1
    helpers = (HELP_T_6.get(zs, ()), HELP_T.get(zs, ()))

    def chip(x, y, z):
        return ((x * 2 + y % 2) * zs + z, (y // 2) * 2 + core)

    def after(place):
        dp, group = place
        return ((dp + group // 6) % dps, (group + 2) % 8)

    def relay(x, y, z):
        turn = jnp.where((z == zs - 1) & (y == 6), 1, 0)
        return chip(x, (y + Y - 3 + turn) % Y, z)

    source = chip(x, (y + 3 - jnp.where(last & (y == 4), 1, 0)) % Y, z)
    previous = ((dp + dps - (7 - group) // 6) % dps, (group + 6) % 8)
    p_dp, p_group = previous
    p_z = p_dp % zs
    p_y = (p_group // 2) * 2 + (p_dp // zs) % 2
    helper = z < 0
    for low in (0, 1):
        for z_j in helpers[1 - low]:
            helper = helper | ((y == low) & (z == z_j))
    helped = chip(x, 7 - y, zs - 1)
    p_x = p_dp // (2 * zs)
    return dict(
        core=core,
        z=z,
        short=last & (y == 7),
        long=last & (y == 6),
        long_end=(p_z == zs - 1) & (p_y == 6),
        y=y,
        idle=last & (y == 3),
        end=(p_z == zs - 1) & (p_y == 7),
        late=(p_z == zs - 1) & (p_y >= 6),
        helper=helper,
        mate=(dp, group + 1 - 2 * core),
        after=after((dp, group)),
        previous=previous,
        via=relay(x, y, z),
        source=source,
        onward=after(source),
        previous_via=relay(p_dp // (2 * zs), p_y, p_z),
        helped=helped,
        help_end=after(helped),
        helpers=[[chip(x, 1 - k, z_j) for z_j in zz] for k, zz in enumerate(helpers)],
        end_helpers=[[chip(p_x, 1 - k, z_j) for z_j in zz] for k, zz in enumerate(helpers)],
    )


def kernel(
    zs,
    dps,
    log_scale_hbm,
    bias_hbm,
    image_hbm,
    text_hbm,
    accum_hbm,
    ids_hbm,
    loss_hbm,
    image_grad_hbm,
    text_grad_top,
    text_grad_bottom,
    image,
    text,
    accum,
    own,
    mate_text,
    far_text,
    coef,
    grad,
    part,
    mate_part,
    total,
    carried,
    far_carried,
    passing,
    loss,
    loss_row,
    image_grad,
    ids,
    mate_ids,
    far_ids,
    log_scale,
    bias,
    load_sem,
    store_sem,
    sends,
    recvs,
):
    at = places(zs, dps)
    core = at["core"]
    is0 = core == 0
    is1 = core == 1
    short, idle, end, helper = at["short"], at["idle"], at["end"], at["helper"]
    helpers = (HELP_T_6.get(zs, ()), HELP_T.get(zs, ()))
    barrier = pltpu.get_barrier_semaphore()

    def greet(place):
        pl.semaphore_signal(barrier, inc=1, device_id=place, device_id_type=MESH)

    greet(at["mate"])
    greet(at["previous"])

    @pl.when(jnp.logical_not(idle))
    def _():
        greet(at["source"])

    @pl.when(jnp.logical_not(end))
    def _():
        greet(at["previous_via"])

    if helpers[1]:

        @pl.when(at["long_end"])
        def _():
            for place in at["end_helpers"][0]:
                greet(place)

        @pl.when(end)
        def _():
            for place in at["end_helpers"][1]:
                greet(place)

        @pl.when(helper)
        def _():
            greet(at["helped"])

    partners = 2 + jnp.where(short, len(helpers[1]), 1) + jnp.where(at["long"], len(helpers[0]), 0)
    partners += jnp.where(idle, 0, 1) + jnp.where(helper, 1, 0)

    loads = [
        pltpu.make_async_copy(src, dst, load_sem.at[i])
        for i, (src, dst) in enumerate(
            [
                (text_hbm, text),
                (image_hbm, image),
                (ids_hbm, ids),
                (log_scale_hbm, log_scale),
                (bias_hbm, bias),
                (accum_hbm, accum),
            ]
        )
    ]
    for copy in loads:
        copy.start()

    count = [0]

    def fresh():
        count[0] += 1
        return count[0] - 1

    def remote(src, dst, to, send=None, recv=None):
        k = fresh() if send is None or recv is None else 0
        return pltpu.make_async_remote_copy(
            src_ref=src,
            dst_ref=dst,
            send_sem=sends.at[k if send is None else send],
            recv_sem=recvs.at[k if recv is None else recv],
            device_id=at[to] if isinstance(to, str) else to,
            device_id_type=MESH,
        )

    def rows(ref, piece, shift=0):
        return ref.at[pl.ds(piece[0] + shift, piece[1])]

    room = [0]

    def slot(n):
        room[0] += n
        return passing.at[pl.ds(room[0] - n, n)]

    class Stream:
        def __init__(self, src, dst, ahead, back, help_z, help_z_6=()):
            self.ahead, self.back = ahead, back
            ahead_ids = [fresh() for _ in ahead]
            leg1_ids = [fresh() for _ in back]
            leg2_ids = [fresh() for _ in back]
            self.straight = [
                remote(rows(src, p), rows(dst, p), "after", k, k) for p, k in zip(ahead, ahead_ids)
            ]
            slots = [slot(n) for _, n in back]
            self.leg1 = [
                remote(rows(src, p), t, "via", k, k) for p, t, k in zip(back, slots, leg1_ids)
            ]
            self.leg2 = [
                remote(t, rows(dst, p), "onward", k, k) for p, t, k in zip(back, slots, leg2_ids)
            ]
            self.instead = [
                remote(rows(src, p), rows(dst, p), "after", k1, k2)
                for p, k1, k2 in zip(back, leg1_ids, leg2_ids)
            ]
            self.help1, self.help2, self.help_z = [], [], help_z
            self.six1, self.six2, self.help_z_6 = {}, {}, help_z_6
            if help_z:
                marks = list(zip(back, leg1_ids, leg2_ids)) + list(zip(ahead, ahead_ids, ahead_ids))
                marks = marks[: len(help_z)]
                k, spot = fresh(), room[0]
                slot(max(p[1] for p, _, _ in marks))

                def pair(p, k1, k2, place):
                    here = passing.at[pl.ds(spot, p[1])]
                    return (
                        remote(rows(src, p), here, place, k1, k),
                        remote(here, rows(dst, p), "help_end", k, k2),
                    )

                for j, (p, k1, k2) in enumerate(marks):
                    one, two = pair(p, k1, k2, at["helpers"][1][j])
                    self.help1.append(one)
                    self.help2.append(two)
                for j in range(len(help_z_6)):
                    i = len(ahead) - 1 - j
                    place = at["helpers"][0][j]
                    self.six1[i], self.six2[i] = pair(ahead[i], ahead_ids[i], ahead_ids[i], place)

        def send_ahead(self, i, helped=True):
            straight = None
            j = len(self.back) + i
            if j < len(self.help1):
                straight = jnp.logical_not(short)
                if helped:

                    @pl.when(short)
                    def _():
                        self.help1[j].start()

            if i in self.six1:
                long = at["long"]
                other = jnp.logical_not(long)
                straight = other if straight is None else straight & other

                @pl.when(long)
                def _():
                    self.six1[i].start()

            if straight is None:
                self.straight[i].start()
            else:

                @pl.when(straight)
                def _():
                    self.straight[i].start()

        def send_back(self, i):
            @pl.when(short)
            def _():
                (self.help1 if self.help1 else self.instead)[i].start()

            @pl.when(jnp.logical_not(short))
            def _():
                self.leg1[i].start()

        def relay(self, i):
            @pl.when(jnp.logical_not(idle))
            def _():
                self.leg1[i].wait_recv()
                self.leg2[i].start()

        def each_helper(self, act):
            for z_j, one, two in zip(self.help_z, self.help1, self.help2):

                @pl.when((at["y"] == 0) & (at["z"] == z_j))
                def _():
                    act(one, two)

            for z_j, one, two in zip(self.help_z_6, self.six1.values(), self.six2.values()):

                @pl.when((at["y"] == 1) & (at["z"] == z_j))
                def _():
                    act(one, two)

        def help(self):
            def act(one, two):
                one.wait_recv()
                two.start()

            self.each_helper(act)

        def wait_sends(self):
            for copy in self.straight + self.leg1:
                copy.wait_send()

            @pl.when(jnp.logical_not(idle))
            def _():
                for copy in self.leg2:
                    copy.wait_send()

            self.each_helper(lambda one, two: two.wait_send())

    texts = Stream(
        own, far_text, AHEAD_T, BACK_T, HELP_T.get(zs, ()), HELP_T_6.get(zs, ())
    )
    carries = Stream(
        carried, far_carried, AHEAD_C, BACK_C, HELP_C.get(zs, ()), HELP_C_6.get(zs, ())
    )
    ids_ahead = remote(ids, far_ids, "after")
    text_down = remote(own, mate_text, "mate")
    ids_down = remote(ids, mate_ids, "mate")
    arrivals = list(zip(texts.straight, AHEAD_T)) + list(zip(texts.leg2, BACK_T))
    text_up = [remote(rows(far_text, p), rows(mate_text, p), "mate") for _, p in arrivals]
    ids_up = remote(far_ids, mate_ids, "mate")
    part_over = remote(part, mate_part, "mate")

    def terms(text_block, text_ids, first, out):
        scale = jnp.exp(jnp.full((1, 256), log_scale[0], jnp.float32))
        shift = bias[0]
        image_ids = jnp.transpose(jnp.broadcast_to(ids[...].astype(jnp.float32), (128, 256)))
        other = text_ids[...].astype(jnp.float32)
        for i in range(2):
            at_rows = pl.ds(128 * i, 128)
            logits = (
                scale
                * lax.dot_general(
                    image[at_rows, :],
                    text_block[...],
                    (((1,), (1,)), ((), ())),
                    preferred_element_type=jnp.float32,
                )
                + shift
            )
            mine = image_ids[128 * i : 128 * (i + 1), 0:1]
            minus = jnp.where(mine == other, -1.0, 1.0)
            u = minus * logits
            e = jnp.exp(-jnp.abs(u))
            soft = jnp.maximum(u, 0.0) + jnp.log1p(e)
            sig = jnp.where(u >= 0, 1.0, e) / (1.0 + e)
            coef[at_rows, :] = (minus * sig * scale).astype(jnp.bfloat16)
            folded = soft[:, :128] + soft[:, 128:]
            if first:
                loss[at_rows, :] = folded
            else:
                loss[at_rows, :] = loss[at_rows, :] + folded
        for j in range(image.shape[1] // TILE):
            cols = pl.ds(TILE * j, TILE)
            g = jnp.dot(coef[...], text_block[:, cols], preferred_element_type=jnp.float32)
            if first:
                grad[:, cols] = g
            else:
                grad[:, cols] = grad[:, cols] + g
            out[:, cols] = lax.dot_general(
                coef[...],
                image[:, cols],
                (((0,), (0,)), ((), ())),
                preferred_element_type=jnp.float32,
            )

    loads[0].wait()
    own[...] = text[...].astype(jnp.bfloat16)
    for copy in loads[1:5]:
        copy.wait()
    terms(own, ids, True, total)
    loads[5].wait()

    @pl.when(is1)
    def _():
        carried[...] = (total[...] + accum[...]).astype(jnp.bfloat16)

    pl.semaphore_wait(barrier, partners)

    for i in range(max(len(BACK_T), len(AHEAD_T))):
        if i < len(BACK_T):
            texts.send_back(i)
        if i < len(AHEAD_T):
            texts.send_ahead(i)
        if i == 0:
            ids_ahead.start()

            @pl.when(is0)
            def _():
                text_down.start()
                ids_down.start()

    @pl.when(is1)
    def _():
        text_down.wait_recv()
        ids_down.wait_recv()
        terms(mate_text, mate_ids, False, part)
        part_over.start()

    @pl.when(is0)
    def _():
        part_over.wait_recv()
        carried[...] = (total[...] + accum[...] + mate_part[...]).astype(jnp.bfloat16)

    @pl.when(short)
    def _():
        for copy in carries.help1 or carries.instead:
            copy.start()

    for i in range(len(AHEAD_C)):
        carries.send_ahead(i, helped=False)
    for i in range(max(len(BACK_T), len(BACK_C))):
        if i < len(BACK_T):
            texts.relay(i)
        if i < len(BACK_C):

            @pl.when(jnp.logical_not(short))
            def _():
                carries.leg1[i].start()
    texts.help()

    ids_ahead.wait_recv()

    @pl.when(is1)
    def _():
        ids_up.start()

    def relay_carries(first, end):
        for i in range(first, end):
            carries.relay(i)

    half = len(BACK_C) // 2
    relay_carries(0, half)
    carries.help()
    relay_carries(half, len(BACK_C))

    for i, (copy, _) in enumerate(arrivals):
        copy.wait_recv()

        @pl.when(is1)
        def _():
            text_up[i].start()

    @pl.when(is0)
    def _():
        ids_up.wait_recv()
        for copy in text_up:
            copy.wait_recv()
        terms(mate_text, mate_ids, False, part)
        part_over.start()

    terms(far_text, far_ids, False, total)

    image_grad[...] = grad[...].astype(jnp.bfloat16)
    store_image = pltpu.make_async_copy(image_grad, image_grad_hbm, store_sem.at[0])
    store_image.start()
    columns = (SHIFTS + 1) * image.shape[0]
    loss_row[...] = jnp.sum(jnp.transpose(loss[...]), axis=0, keepdims=True) / columns
    store_loss = pltpu.make_async_copy(loss_row, loss_hbm, store_sem.at[1])
    store_loss.start()

    @pl.when(is1)
    def _():
        part_over.wait_recv()
        total[...] = total[...] + mate_part[...]

    stores = []

    def finish(copy, piece):
        copy.wait_recv()
        at_rows = pl.ds(piece[0], piece[1])
        total[at_rows, :] = total[at_rows, :] + far_carried[at_rows, :].astype(jnp.float32)
        middle = total.shape[0] // 2
        top = piece[0] < middle
        place = rows(text_grad_top, piece) if top else rows(text_grad_bottom, piece, -middle)
        store = pltpu.make_async_copy(rows(total, piece), place, store_sem.at[2 + len(stores)])
        store.start()
        stores.append(store)

    half = len(AHEAD_C) - len(BACK_C)
    for i in range(half):
        finish(carries.straight[i], AHEAD_C[i])
    for i in range(len(BACK_C)):
        finish(carries.leg2[i], BACK_C[i])
        finish(carries.straight[half + i], AHEAD_C[half + i])

    texts.wait_sends()
    carries.wait_sends()
    ids_ahead.wait_send()
    part_over.wait_send()

    @pl.when(is0)
    def _():
        text_down.wait_send()
        ids_down.wait_send()

    @pl.when(is1)
    def _():
        ids_up.wait_send()
        for copy in text_up:
            copy.wait_send()

    store_image.wait()
    store_loss.wait()
    for store in stores:
        store.wait()


def store_kernel(loss, image_grad, top, bottom, loss_hbm, image_grad_hbm, text_grad_hbm, sem):
    middle = top.shape[0]
    pairs = [
        (top, text_grad_hbm.at[pl.ds(0, middle)]),
        (bottom, text_grad_hbm.at[pl.ds(middle, middle)]),
        (image_grad, image_grad_hbm),
        (loss, loss_hbm),
    ]
    copies = [pltpu.make_async_copy(src, dst, sem.at[i]) for i, (src, dst) in enumerate(pairs)]
    for copy in copies:
        copy.start()
    for copy in copies:
        copy.wait()


def solution(mesh):
    dps = mesh.shape["dp"]
    zs = max(dps // 8, 1)
    copies = 3 * len(BACK_T) + 2 * len(AHEAD_T) + len(AHEAD_C) + 2 * len(BACK_C) + 5
    copies += 2
    pieces = len(AHEAD_C) + len(BACK_C)
    passing_rows = sum(n for _, n in BACK_T) + sum(n for _, n in BACK_C)
    passing_rows += 32 + 32

    def body(image_emb, text_emb, text_accum, pair_ids, log_scale, bias):
        n, d = image_emb.shape
        any_space = pl.BlockSpec(memory_space=pl.ANY)
        hbm = pl.BlockSpec(memory_space=pltpu.HBM)
        f32, bf16, i32 = jnp.float32, jnp.bfloat16, jnp.int32
        shapes = (
            jax.ShapeDtypeStruct((1, n), f32),
            jax.ShapeDtypeStruct((n, d), bf16),
            jax.ShapeDtypeStruct((n, d), f32),
        )
        results = pl.pallas_call(
            functools.partial(kernel, zs, dps),
            out_shape=shapes[:2] + (jax.ShapeDtypeStruct((n // 2, d), f32),) * 2,
            in_specs=[hbm] * 6,
            out_specs=(any_space,) * 4,
            scratch_shapes=[
                pltpu.VMEM((n, d), bf16),
                pltpu.VMEM((n, d), f32),
                pltpu.VMEM((n, d), f32),
                pltpu.VMEM((n, d), bf16),
                pltpu.VMEM((n, d), bf16),
                pltpu.VMEM((n, d), bf16),
                pltpu.VMEM((n, n), bf16),
                pltpu.VMEM((n, d), f32),
                pltpu.VMEM((n, d), f32),
                pltpu.VMEM((n, d), f32),
                pltpu.VMEM((n, d), f32),
                pltpu.VMEM((n, d), bf16),
                pltpu.VMEM((n, d), bf16),
                pltpu.VMEM((passing_rows, d), bf16),
                pltpu.VMEM((n, 128), f32),
                pltpu.VMEM((1, n), f32),
                pltpu.VMEM((n, d), bf16),
                pltpu.VMEM((1, n), i32),
                pltpu.VMEM((1, n), i32),
                pltpu.VMEM((1, n), i32),
                pltpu.SMEM((1,), f32),
                pltpu.SMEM((1,), f32),
                pltpu.SemaphoreType.DMA((6,)),
                pltpu.SemaphoreType.DMA((2 + pieces,)),
                pltpu.SemaphoreType.DMA((copies,)),
                pltpu.SemaphoreType.DMA((copies,)),
            ],
            compiler_params=pltpu.CompilerParams(
                collective_id=0, has_side_effects=True, vmem_limit_bytes=53120 << 10
            ),
        )(log_scale, bias, image_emb, text_emb, text_accum, pair_ids.reshape(1, n))
        loss, image_grad, text_grad = pl.pallas_call(
            store_kernel,
            out_shape=shapes,
            in_specs=[any_space] * 4,
            out_specs=(hbm, hbm, hbm),
            scratch_shapes=[pltpu.SemaphoreType.DMA((4,))],
            compiler_params=pltpu.CompilerParams(vmem_limit_bytes=1 << 20),
        )(*results)
        return loss.reshape(n), image_grad, text_grad

    split = P(("dp", "group"))
    wide = P(("dp", "group"), None)
    return jax.shard_map(
        body,
        mesh=mesh,
        in_specs=(wide, wide, wide, split, P(), P()),
        out_specs=(split, wide, wide),
        check_vma=False,
    )
```

```python
import functools

import jax
import jax.numpy as jnp
from jax import lax
from jax.experimental import pallas as pl
from jax.experimental.pallas import tpu as pltpu
from jax.sharding import PartitionSpec as P

SHIFTS = 2
Y = 8
TILE = 384
MESH = pl.DeviceIdType.MESH

AHEAD_T = [(64 + 32 * i, 32) for i in range(6)]
BACK_T = [(16 * i, 16) for i in range(4)]
AHEAD_C = [(48, 16)] + [(64 + 32 * i, 32) for i in range(5)] + [(224, 16), (240, 16)]
BACK_C = [(16 * i, 16) for i in range(3)]
HELP_T = {12: (1, 2, 3, 4, 5, 6, 7)}
HELP_C = {12: (1, 2, 3, 4, 5, 6)}
HELP_T_6 = {12: (1, 2, 3, 4)}
HELP_C_6 = {12: (1, 2, 3)}


def places(zs, dps):
    dp = lax.axis_index("dp")
    group = lax.axis_index("group")
    xs = max(dps // (2 * zs), 1)
    core = group % 2
    z = dp % zs
    y = (group // 2) * 2 + (dp // zs) % 2
    x = dp // (2 * zs)
    last = z == zs - 1
    helpers = (HELP_T_6.get(zs, ()), HELP_T.get(zs, ()))

    def chip(x, y, z):
        return ((x * 2 + y % 2) * zs + z, (y // 2) * 2 + core)

    def after(place):
        dp, group = place
        return ((dp + group // 6) % dps, (group + 2) % 8)

    def relay(x, y, z):
        turn = jnp.where((z == zs - 1) & (y == 6), 1, 0)
        return chip(x, (y + Y - 3 + turn) % Y, z)

    source = chip(x, (y + 3 - jnp.where(last & (y == 4), 1, 0)) % Y, z)
    previous = ((dp + dps - (7 - group) // 6) % dps, (group + 6) % 8)
    p_dp, p_group = previous
    p_z = p_dp % zs
    p_y = (p_group // 2) * 2 + (p_dp // zs) % 2
    helper = z < 0
    for low in (0, 1):
        for z_j in helpers[1 - low]:
            helper = helper | ((y == low) & (z == z_j))
    helped = chip(x, 7 - y, zs - 1)
    p_x = p_dp // (2 * zs)
    return dict(
        core=core,
        z=z,
        short=last & (y == 7),
        long=last & (y == 6),
        long_end=(p_z == zs - 1) & (p_y == 6),
        y=y,
        idle=last & (y == 3),
        end=(p_z == zs - 1) & (p_y == 7),
        late=(p_z == zs - 1) & (p_y >= 6),
        helper=helper,
        mate=(dp, group + 1 - 2 * core),
        after=after((dp, group)),
        previous=previous,
        via=relay(x, y, z),
        source=source,
        onward=after(source),
        previous_via=relay(p_dp // (2 * zs), p_y, p_z),
        helped=helped,
        help_end=after(helped),
        helpers=[[chip(x, 1 - k, z_j) for z_j in zz] for k, zz in enumerate(helpers)],
        end_helpers=[[chip(p_x, 1 - k, z_j) for z_j in zz] for k, zz in enumerate(helpers)],
    )


def kernel(
    zs,
    dps,
    log_scale_hbm,
    bias_hbm,
    image_hbm,
    text_hbm,
    accum_hbm,
    ids_hbm,
    loss_hbm,
    image_grad_hbm,
    text_grad_top,
    text_grad_bottom,
    image,
    text,
    accum,
    own,
    mate_text,
    far_text,
    coef,
    grad,
    part,
    mate_part,
    total,
    carried,
    far_carried,
    passing,
    loss,
    loss_row,
    image_grad,
    ids,
    mate_ids,
    far_ids,
    log_scale,
    bias,
    load_sem,
    store_sem,
    sends,
    recvs,
):
    at = places(zs, dps)
    core = at["core"]
    is0 = core == 0
    is1 = core == 1
    short, idle, end, helper = at["short"], at["idle"], at["end"], at["helper"]
    helpers = (HELP_T_6.get(zs, ()), HELP_T.get(zs, ()))
    barrier = pltpu.get_barrier_semaphore()

    def greet(place):
        pl.semaphore_signal(barrier, inc=1, device_id=place, device_id_type=MESH)

    greet(at["mate"])
    greet(at["previous"])

    @pl.when(jnp.logical_not(idle))
    def _():
        greet(at["source"])

    @pl.when(jnp.logical_not(end))
    def _():
        greet(at["previous_via"])

    if helpers[1]:

        @pl.when(at["long_end"])
        def _():
            for place in at["end_helpers"][0]:
                greet(place)

        @pl.when(end)
        def _():
            for place in at["end_helpers"][1]:
                greet(place)

        @pl.when(helper)
        def _():
            greet(at["helped"])

    partners = 2 + jnp.where(short, len(helpers[1]), 1) + jnp.where(at["long"], len(helpers[0]), 0)
    partners += jnp.where(idle, 0, 1) + jnp.where(helper, 1, 0)

    loads = [
        pltpu.make_async_copy(src, dst, load_sem.at[i])
        for i, (src, dst) in enumerate(
            [
                (text_hbm, text),
                (image_hbm, image),
                (ids_hbm, ids),
                (log_scale_hbm, log_scale),
                (bias_hbm, bias),
                (accum_hbm, accum),
            ]
        )
    ]
    for copy in loads:
        copy.start()

    count = [0]

    def fresh():
        count[0] += 1
        return count[0] - 1

    def remote(src, dst, to, send=None, recv=None):
        k = fresh() if send is None or recv is None else 0
        return pltpu.make_async_remote_copy(
            src_ref=src,
            dst_ref=dst,
            send_sem=sends.at[k if send is None else send],
            recv_sem=recvs.at[k if recv is None else recv],
            device_id=at[to] if isinstance(to, str) else to,
            device_id_type=MESH,
        )

    def rows(ref, piece, shift=0):
        return ref.at[pl.ds(piece[0] + shift, piece[1])]

    room = [0]

    def slot(n):
        room[0] += n
        return passing.at[pl.ds(room[0] - n, n)]

    class Stream:
        def __init__(self, src, dst, ahead, back, help_z, help_z_6=()):
            self.ahead, self.back = ahead, back
            ahead_ids = [fresh() for _ in ahead]
            leg1_ids = [fresh() for _ in back]
            leg2_ids = [fresh() for _ in back]
            self.straight = [
                remote(rows(src, p), rows(dst, p), "after", k, k) for p, k in zip(ahead, ahead_ids)
            ]
            slots = [slot(n) for _, n in back]
            self.leg1 = [
                remote(rows(src, p), t, "via", k, k) for p, t, k in zip(back, slots, leg1_ids)
            ]
            self.leg2 = [
                remote(t, rows(dst, p), "onward", k, k) for p, t, k in zip(back, slots, leg2_ids)
            ]
            self.instead = [
                remote(rows(src, p), rows(dst, p), "after", k1, k2)
                for p, k1, k2 in zip(back, leg1_ids, leg2_ids)
            ]
            self.help1, self.help2, self.help_z = [], [], help_z
            self.six1, self.six2, self.help_z_6 = {}, {}, help_z_6
            if help_z:
                marks = list(zip(back, leg1_ids, leg2_ids)) + list(zip(ahead, ahead_ids, ahead_ids))
                marks = marks[: len(help_z)]
                k, spot = fresh(), room[0]
                slot(max(p[1] for p, _, _ in marks))

                def pair(p, k1, k2, place):
                    here = passing.at[pl.ds(spot, p[1])]
                    return (
                        remote(rows(src, p), here, place, k1, k),
                        remote(here, rows(dst, p), "help_end", k, k2),
                    )

                for j, (p, k1, k2) in enumerate(marks):
                    one, two = pair(p, k1, k2, at["helpers"][1][j])
                    self.help1.append(one)
                    self.help2.append(two)
                for j in range(len(help_z_6)):
                    i = len(ahead) - 1 - j
                    place = at["helpers"][0][j]
                    self.six1[i], self.six2[i] = pair(ahead[i], ahead_ids[i], ahead_ids[i], place)

        def send_ahead(self, i, helped=True):
            straight = None
            j = len(self.back) + i
            if j < len(self.help1):
                straight = jnp.logical_not(short)
                if helped:

                    @pl.when(short)
                    def _():
                        self.help1[j].start()

            if i in self.six1:
                long = at["long"]
                other = jnp.logical_not(long)
                straight = other if straight is None else straight & other

                @pl.when(long)
                def _():
                    self.six1[i].start()

            if straight is None:
                self.straight[i].start()
            else:

                @pl.when(straight)
                def _():
                    self.straight[i].start()

        def send_back(self, i):
            @pl.when(short)
            def _():
                (self.help1 if self.help1 else self.instead)[i].start()

            @pl.when(jnp.logical_not(short))
            def _():
                self.leg1[i].start()

        def relay(self, i):
            @pl.when(jnp.logical_not(idle))
            def _():
                self.leg1[i].wait_recv()
                self.leg2[i].start()

        def each_helper(self, act):
            for z_j, one, two in zip(self.help_z, self.help1, self.help2):

                @pl.when((at["y"] == 0) & (at["z"] == z_j))
                def _():
                    act(one, two)

            for z_j, one, two in zip(self.help_z_6, self.six1.values(), self.six2.values()):

                @pl.when((at["y"] == 1) & (at["z"] == z_j))
                def _():
                    act(one, two)

        def help(self):
            def act(one, two):
                one.wait_recv()
                two.start()

            self.each_helper(act)

        def wait_sends(self):
            for copy in self.straight + self.leg1:
                copy.wait_send()

            @pl.when(jnp.logical_not(idle))
            def _():
                for copy in self.leg2:
                    copy.wait_send()

            self.each_helper(lambda one, two: two.wait_send())

    texts = Stream(
        own, far_text, AHEAD_T, BACK_T, HELP_T.get(zs, ()), HELP_T_6.get(zs, ())
    )
    carries = Stream(
        carried, far_carried, AHEAD_C, BACK_C, HELP_C.get(zs, ()), HELP_C_6.get(zs, ())
    )
    ids_ahead = remote(ids, far_ids, "after")
    text_down = remote(own, mate_text, "mate")
    ids_down = remote(ids, mate_ids, "mate")
    arrivals = list(zip(texts.straight, AHEAD_T)) + list(zip(texts.leg2, BACK_T))
    text_up = [remote(rows(far_text, p), rows(mate_text, p), "mate") for _, p in arrivals]
    ids_up = remote(far_ids, mate_ids, "mate")
    part_over = remote(part, mate_part, "mate")

    def terms(text_block, text_ids, first, out):
        scale = jnp.exp(jnp.full((1, 256), log_scale[0], jnp.float32))
        shift = bias[0]
        image_ids = jnp.transpose(jnp.broadcast_to(ids[...].astype(jnp.float32), (128, 256)))
        other = text_ids[...].astype(jnp.float32)
        for i in range(2):
            at_rows = pl.ds(128 * i, 128)
            logits = (
                scale
                * lax.dot_general(
                    image[at_rows, :],
                    text_block[...],
                    (((1,), (1,)), ((), ())),
                    preferred_element_type=jnp.float32,
                )
                + shift
            )
            mine = image_ids[128 * i : 128 * (i + 1), 0:1]
            minus = jnp.where(mine == other, -1.0, 1.0)
            u = minus * logits
            e = jnp.exp(-jnp.abs(u))
            soft = jnp.maximum(u, 0.0) + jnp.log1p(e)
            sig = jnp.where(u >= 0, 1.0, e) / (1.0 + e)
            coef[at_rows, :] = (minus * sig * scale).astype(jnp.bfloat16)
            folded = soft[:, :128] + soft[:, 128:]
            if first:
                loss[at_rows, :] = folded
            else:
                loss[at_rows, :] = loss[at_rows, :] + folded
        for j in range(image.shape[1] // TILE):
            cols = pl.ds(TILE * j, TILE)
            g = jnp.dot(coef[...], text_block[:, cols], preferred_element_type=jnp.float32)
            if first:
                grad[:, cols] = g
            else:
                grad[:, cols] = grad[:, cols] + g
            out[:, cols] = lax.dot_general(
                coef[...],
                image[:, cols],
                (((0,), (0,)), ((), ())),
                preferred_element_type=jnp.float32,
            )

    loads[0].wait()
    own[...] = text[...].astype(jnp.bfloat16)
    for copy in loads[1:5]:
        copy.wait()
    terms(own, ids, True, total)
    loads[5].wait()

    @pl.when(is1)
    def _():
        carried[...] = (total[...] + accum[...]).astype(jnp.bfloat16)

    pl.semaphore_wait(barrier, partners)

    for i in range(max(len(BACK_T), len(AHEAD_T))):
        if i < len(BACK_T):
            texts.send_back(i)
        if i < len(AHEAD_T):
            texts.send_ahead(i)
        if i == 0:
            ids_ahead.start()

            @pl.when(is0)
            def _():
                text_down.start()
                ids_down.start()

    @pl.when(is1)
    def _():
        text_down.wait_recv()
        ids_down.wait_recv()
        terms(mate_text, mate_ids, False, part)
        part_over.start()

    @pl.when(is0)
    def _():
        part_over.wait_recv()
        carried[...] = (total[...] + accum[...] + mate_part[...]).astype(jnp.bfloat16)

    @pl.when(short)
    def _():
        for copy in carries.help1 or carries.instead:
            copy.start()

    for i in range(len(AHEAD_C)):
        carries.send_ahead(i, helped=False)
    for i in range(max(len(BACK_T), len(BACK_C))):
        if i < len(BACK_T):
            texts.relay(i)
        if i < len(BACK_C):

            @pl.when(jnp.logical_not(short))
            def _():
                carries.leg1[i].start()
    texts.help()

    ids_ahead.wait_recv()

    @pl.when(is1)
    def _():
        ids_up.start()

    def relay_carries(first, end):
        for i in range(first, end):
            carries.relay(i)

    half = len(BACK_C) // 2
    relay_carries(0, half)
    carries.help()
    relay_carries(half, len(BACK_C))

    for i, (copy, _) in enumerate(arrivals):
        copy.wait_recv()

        @pl.when(is1)
        def _():
            text_up[i].start()

    @pl.when(is0)
    def _():
        ids_up.wait_recv()
        for copy in text_up:
            copy.wait_recv()
        terms(mate_text, mate_ids, False, part)
        part_over.start()

    terms(far_text, far_ids, False, total)

    image_grad[...] = grad[...].astype(jnp.bfloat16)
    store_image = pltpu.make_async_copy(image_grad, image_grad_hbm, store_sem.at[0])
    store_image.start()
    columns = (SHIFTS + 1) * image.shape[0]
    loss_row[...] = jnp.sum(jnp.transpose(loss[...]), axis=0, keepdims=True) / columns
    store_loss = pltpu.make_async_copy(loss_row, loss_hbm, store_sem.at[1])
    store_loss.start()

    @pl.when(is1)
    def _():
        part_over.wait_recv()
        total[...] = total[...] + mate_part[...]

    stores = []

    def finish(copy, piece):
        copy.wait_recv()
        at_rows = pl.ds(piece[0], piece[1])
        total[at_rows, :] = total[at_rows, :] + far_carried[at_rows, :].astype(jnp.float32)
        middle = total.shape[0] // 2
        top = piece[0] < middle
        place = rows(text_grad_top, piece) if top else rows(text_grad_bottom, piece, -middle)
        store = pltpu.make_async_copy(rows(total, piece), place, store_sem.at[2 + len(stores)])
        store.start()
        stores.append(store)

    half = len(AHEAD_C) - len(BACK_C)
    for i in range(half):
        finish(carries.straight[i], AHEAD_C[i])
    for i in range(len(BACK_C)):
        finish(carries.leg2[i], BACK_C[i])
        finish(carries.straight[half + i], AHEAD_C[half + i])

    texts.wait_sends()
    carries.wait_sends()
    ids_ahead.wait_send()
    part_over.wait_send()

    @pl.when(is0)
    def _():
        text_down.wait_send()
        ids_down.wait_send()

    @pl.when(is1)
    def _():
        ids_up.wait_send()
        for copy in text_up:
            copy.wait_send()

    store_image.wait()
    store_loss.wait()
    for store in stores:
        store.wait()


def store_kernel(loss, image_grad, top, bottom, loss_hbm, image_grad_hbm, text_grad_hbm, sem):
    middle = top.shape[0]
    pairs = [
        (top, text_grad_hbm.at[pl.ds(0, middle)]),
        (bottom, text_grad_hbm.at[pl.ds(middle, middle)]),
        (image_grad, image_grad_hbm),
        (loss, loss_hbm),
    ]
    copies = [pltpu.make_async_copy(src, dst, sem.at[i]) for i, (src, dst) in enumerate(pairs)]
    for copy in copies:
        copy.start()
    for copy in copies:
        copy.wait()


def solution(mesh):
    dps = mesh.shape["dp"]
    zs = max(dps // 8, 1)
    copies = 3 * len(BACK_T) + 2 * len(AHEAD_T) + len(AHEAD_C) + 2 * len(BACK_C) + 5
    copies += 2
    pieces = len(AHEAD_C) + len(BACK_C)
    passing_rows = sum(n for _, n in BACK_T) + sum(n for _, n in BACK_C)
    passing_rows += 32 + 32

    def body(image_emb, text_emb, text_accum, pair_ids, log_scale, bias):
        n, d = image_emb.shape
        any_space = pl.BlockSpec(memory_space=pl.ANY)
        hbm = pl.BlockSpec(memory_space=pltpu.HBM)
        f32, bf16, i32 = jnp.float32, jnp.bfloat16, jnp.int32
        shapes = (
            jax.ShapeDtypeStruct((1, n), f32),
            jax.ShapeDtypeStruct((n, d), bf16),
            jax.ShapeDtypeStruct((n, d), f32),
        )
        results = pl.pallas_call(
            functools.partial(kernel, zs, dps),
            out_shape=shapes[:2] + (jax.ShapeDtypeStruct((n // 2, d), f32),) * 2,
            in_specs=[hbm] * 6,
            out_specs=(any_space,) * 4,
            scratch_shapes=[
                pltpu.VMEM((n, d), bf16),
                pltpu.VMEM((n, d), f32),
                pltpu.VMEM((n, d), f32),
                pltpu.VMEM((n, d), bf16),
                pltpu.VMEM((n, d), bf16),
                pltpu.VMEM((n, d), bf16),
                pltpu.VMEM((n, n), bf16),
                pltpu.VMEM((n, d), f32),
                pltpu.VMEM((n, d), f32),
                pltpu.VMEM((n, d), f32),
                pltpu.VMEM((n, d), f32),
                pltpu.VMEM((n, d), bf16),
                pltpu.VMEM((n, d), bf16),
                pltpu.VMEM((passing_rows, d), bf16),
                pltpu.VMEM((n, 128), f32),
                pltpu.VMEM((1, n), f32),
                pltpu.VMEM((n, d), bf16),
                pltpu.VMEM((1, n), i32),
                pltpu.VMEM((1, n), i32),
                pltpu.VMEM((1, n), i32),
                pltpu.SMEM((1,), f32),
                pltpu.SMEM((1,), f32),
                pltpu.SemaphoreType.DMA((6,)),
                pltpu.SemaphoreType.DMA((2 + pieces,)),
                pltpu.SemaphoreType.DMA((copies,)),
                pltpu.SemaphoreType.DMA((copies,)),
            ],
            compiler_params=pltpu.CompilerParams(
                collective_id=0, has_side_effects=True, vmem_limit_bytes=53120 << 10
            ),
        )(log_scale, bias, image_emb, text_emb, text_accum, pair_ids.reshape(1, n))
        loss, image_grad, text_grad = pl.pallas_call(
            store_kernel,
            out_shape=shapes,
            in_specs=[any_space] * 4,
            out_specs=(hbm, hbm, hbm),
            scratch_shapes=[pltpu.SemaphoreType.DMA((4,))],
            compiler_params=pltpu.CompilerParams(vmem_limit_bytes=1 << 20),
        )(*results)
        return loss.reshape(n), image_grad, text_grad

    split = P(("dp", "group"))
    wide = P(("dp", "group"), None)
    return jax.shard_map(
        body,
        mesh=mesh,
        in_specs=(wide, wide, wide, split, P(), P()),
        out_specs=(split, wide, wide),
        check_vma=False,
    )
```
